32 devices in a mesh: corner: 8 (over z, x), space: 4 (over y, core).
Axes of the slice: x: 2, y: 2, z: 4, core: 2. Of those that a mesh axis runs over, the one named last changes fastest.
Arguments:
- design: float32 [192, 1024], P('space'), may hold values from 0 to 1
- corner_set: int32 [8], P('corner'), may hold values from 0 to 3
- corner_dose: float32 [8], P('corner'), may hold values from 0.7 to 1.4
- kernel_taps: float32 [4, 4, 8, 17], replicated, may hold values from -1 to 1, as said below
- kernel_weights: float32 [4, 8], replicated, may hold values from 0.1 to 1
- support_mask: int32 [192, 1024], P('space'), may hold values 0 or 1
- load_mask: int32 [192, 1024], P('space'), may hold values 0 or 1
- force: float32 [2], replicated, may hold values from 0.5 to 1.5
Outputs:
- sensitivity: float32 [192, 1024], P('space', 'corner')
The draws below stay inside these ranges and needn't reach their ends.
Inputs may be any that keep to these rules, and one draw needn't show every extreme that they name: `kernel_taps`: entries 0 and 2 along the second dimension lie in 0.2 to 1.
All inputs are finite; a program needn't handle non-finite values. No bound on the sum of `support_mask` or of `load_mask` on one device may be relied on, other than what follows from the above.
Results may differ from the reference program's by a relative error of at most 0.0003.
Values sent between devices are 32-bit elements; how exact they have to be, the bound alone decides.
A program may use at most 128 MiB of HBM per device.

```python
import math
import jax
import jax.numpy as jnp
from jax import lax

NY = 1024
K = 8
RADIUS = 8
NSETS = 4
ITERS = 2
TAPS = 17
CORNERS = 8
NX = 192


def draw_kernel_taps(key, part):
    first, second = jax.random.split(key)
    shape_all = (NSETS, 4, K, TAPS)
    parity = (jnp.arange(4) % 2)[None, :, None, None]
    positive = jax.random.uniform(first, shape_all, jnp.float32, 0.2, 1.0)
    signed = jnp.clip(0.3 * jax.random.normal(second, shape_all, jnp.float32), -1.0, 1.0)
    return jnp.where(parity == 0, positive, signed)


def with_ends(entries, own_key, least, high):
    spot = [jax.random.randint(jax.random.fold_in(own_key, axis), (), 0, length) for axis, length in enumerate(entries.shape)]
    main_axis = entries.shape.index(max(entries.shape))
    beside = spot[:main_axis] + [(spot[main_axis] + 1) % entries.shape[main_axis]] + spot[main_axis + 1:]
    return entries.at[tuple(spot)].set(least).at[tuple(beside)].set(high)


def steps_of(stream_key, dims, cuts, low, high):
    loudness = 1.0
    for axis_at, blocks in cuts:
        heights = jax.random.uniform(jax.random.fold_in(jax.random.fold_in(stream_key, 6), axis_at), (blocks,), jnp.float32, low / len(cuts), high / len(cuts))
        loudness = loudness * jnp.repeat(jnp.exp(heights), dims[axis_at] // blocks).reshape((-1,) + (1,) * (len(dims) - 1 - axis_at))
    return loudness


def setup_inputs(seed: int = 0) -> dict:
    splits = jax.random.split(jax.random.key(seed), 9)
    design = jnp.clip(1.0 * jax.random.uniform(splits[0], (NX, NY), jnp.float32) ** steps_of(splits[0], (NX, NY), ((0, 4),), -0.2, 0.2), 0.0, 1.0)
    corner_set = with_ends(jax.random.randint(splits[1], (CORNERS,), 0, NSETS), jax.random.fold_in(splits[1], 1), 0, NSETS - 1).astype(jnp.int32)
    corner_dose = jnp.clip(jnp.exp(math.log(1.4) - 0.6931472 * jax.random.uniform(splits[2], (CORNERS,), jnp.float32) ** steps_of(splits[2], (CORNERS,), ((0, 8),), -0.2, 0.2)), 0.7, 1.4)
    kernel_taps = draw_kernel_taps(jax.random.fold_in(splits[8], 71), 0)
    kernel_weights = jnp.clip(jnp.exp(jax.random.uniform(splits[4], (NSETS, K), jnp.float32, math.log(0.1), math.log(1.0))), 0.1, 1.0)
    support_mask = with_ends((jax.random.randint(splits[5], (NX, NY), 0, 16) < 1).astype(jnp.int32), jax.random.fold_in(splits[5], 1), 0, 1)
    load_mask = with_ends((jax.random.randint(splits[6], (NX, NY), 0, 8) < 1).astype(jnp.int32), jax.random.fold_in(splits[6], 1), 0, 1)
    force = jnp.clip(jax.random.uniform(splits[7], (2,), jnp.float32, 0.5, 1.5), 0.5, 1.5)
    return {"design": design, "corner_set": corner_set, "corner_dose": corner_dose, "kernel_taps": kernel_taps, "kernel_weights": kernel_weights, "support_mask": support_mask, "load_mask": load_mask, "force": force}


beta_sharp = 8.0
eta_level = 0.25
stiff_floor = 0.05
kappa_ground = 0.1
spring_support = 1.0
poisson_ratio = 0.3


def convolve(part_re, part_im, tap_re, tap_im, along, margin, flipped):
    extent = part_re.shape[along] - 2 * margin
    out_re = 0.0
    out_im = 0.0
    for offset in range(2 * margin + 1):
        begin_at = 2 * margin - offset if flipped else offset
        piece_re = lax.slice_in_dim(part_re, begin_at, begin_at + extent, axis=along)
        out_re = out_re + tap_re[offset] * piece_re
        out_im = out_im + tap_im[offset] * piece_re
        if part_im is not None:
            piece_im = lax.slice_in_dim(part_im, begin_at, begin_at + extent, axis=along)
            out_re = out_re - tap_im[offset] * piece_im
            out_im = out_im + tap_re[offset] * piece_im
    return out_re, out_im


def clear_field(tap_table, weights):
    tap_sums = jnp.sum(tap_table, axis=2)
    row_gain = tap_sums[0] * tap_sums[0] + tap_sums[1] * tap_sums[1]
    col_gain = tap_sums[2] * tap_sums[2] + tap_sums[3] * tap_sums[3]
    return jnp.sum(weights * row_gain * col_gain)


def spread_total():
    return jnp.tanh(beta_sharp * eta_level) + jnp.tanh(beta_sharp * (1.0 - eta_level))


def project(intensity):
    return (jnp.tanh(beta_sharp * eta_level) + jnp.tanh(beta_sharp * (intensity - eta_level))) / spread_total()


def project_slope(intensity):
    inner_tanh = jnp.tanh(beta_sharp * (intensity - eta_level))
    return beta_sharp * (1.0 - inner_tanh * inner_tanh) / spread_total()


def harmonic(lower_side, upper_side):
    return 2.0 * lower_side * upper_side / (lower_side + upper_side)


def coefficients():
    shear = 0.5 * (1.0 - poisson_ratio)
    coef_row = jnp.array([1.0, shear]).reshape(2, 1, 1)
    coef_col = jnp.array([shear, 1.0]).reshape(2, 1, 1)
    return coef_row, coef_col


def operate(field_ext, stiff_ext, ground):
    coef_row, coef_col = coefficients()
    field_all = jnp.pad(field_ext, ((0, 0), (0, 0), (1, 1)))
    stiff_all = jnp.pad(stiff_ext, ((0, 0), (1, 1)))
    stiff_mid = stiff_all[:, 1:-1]
    face_row = harmonic(stiff_mid[:-1], stiff_mid[1:])
    flux_row = coef_row * face_row * (field_all[:, 1:, 1:-1] - field_all[:, :-1, 1:-1])
    stiff_inner = stiff_all[1:-1]
    face_col = harmonic(stiff_inner[:, :-1], stiff_inner[:, 1:])
    flux_col = coef_col * face_col * (field_all[:, 1:-1, 1:] - field_all[:, 1:-1, :-1])
    centre = field_all[:, 1:-1, 1:-1]
    return ground * centre + flux_row[:, :-1] - flux_row[:, 1:] + flux_col[:, :, :-1] - flux_col[:, :, 1:]


def stiffness_slope(field_ext, stiff_ext, field):
    coef_row, coef_col = coefficients()
    field_all = jnp.pad(field_ext, ((0, 0), (0, 0), (1, 1)))
    stiff_all = jnp.pad(stiff_ext, ((0, 0), (1, 1)))
    stiff_mid = stiff_all[:, 1:-1]
    lower_row = stiff_mid[:-1]
    upper_row = stiff_mid[1:]
    diff_row = field_all[:, 1:, 1:-1] - field_all[:, :-1, 1:-1]
    energy_row = jnp.sum(coef_row * diff_row * diff_row, axis=0)
    both_row = lower_row + upper_row
    to_lower = 2.0 * upper_row * upper_row / (both_row * both_row) * energy_row
    to_upper = 2.0 * lower_row * lower_row / (both_row * both_row) * energy_row
    row_part = to_upper[:-1] + to_lower[1:]
    stiff_inner = stiff_all[1:-1]
    lower_col = stiff_inner[:, :-1]
    upper_col = stiff_inner[:, 1:]
    diff_col = field_all[:, 1:-1, 1:] - field_all[:, 1:-1, :-1]
    energy_col = jnp.sum(coef_col * diff_col * diff_col, axis=0)
    both_col = lower_col + upper_col
    left_side = 2.0 * upper_col * upper_col / (both_col * both_col) * energy_col
    right_side = 2.0 * lower_col * lower_col / (both_col * both_col) * energy_col
    col_part = right_side[:, :-1] + left_side[:, 1:]
    return -(kappa_ground * jnp.sum(field * field, axis=0) + row_part + col_part)


def intensity_gain(slope, density, intensity, dose_level, clear_level):
    return slope * (3.0 * (1.0 - stiff_floor)) * density * density * project_slope(intensity) * dose_level / clear_level


def pad_rows(field):
    return jnp.pad(field, ((0, 0), (1, 1), (0, 0)))


def one_corner(design, set_id, dose_level, kernel_taps, kernel_weights, support_mask, load_mask, force):
    tap_table = kernel_taps[set_id]
    weights = kernel_weights[set_id]
    clear_level = clear_field(tap_table, weights)
    design_all = jnp.pad(design, RADIUS)
    fields = []
    intensity = jnp.zeros((NX, NY), jnp.float32)
    for kernel in range(K):
        col_re, col_im = convolve(design_all, None, tap_table[2, kernel], tap_table[3, kernel], 1, RADIUS, True)
        field_re, field_im = convolve(col_re, col_im, tap_table[0, kernel], tap_table[1, kernel], 0, RADIUS, True)
        fields.append((field_re, field_im))
        intensity = intensity + weights[kernel] * (field_re * field_re + field_im * field_im)
    intensity = dose_level * intensity / clear_level
    density = project(intensity)
    stiff = stiff_floor + (1.0 - stiff_floor) * density * density * density
    stiff_ext = jnp.pad(stiff, ((1, 1), (0, 0)))
    ground = kappa_ground * stiff + spring_support * support_mask.astype(jnp.float32)
    load_field = force[:, None, None] * load_mask.astype(jnp.float32)[None]
    solution = jnp.zeros_like(load_field)
    residual = load_field
    direction = load_field
    norm_now = jnp.sum(residual * residual)
    for step in range(ITERS):
        image = operate(pad_rows(direction), stiff_ext, ground)
        alpha = norm_now / jnp.sum(direction * image)
        solution = solution + alpha * direction
        residual = residual - alpha * image
        norm_next = jnp.sum(residual * residual)
        direction = residual + (norm_next / norm_now) * direction
        norm_now = norm_next
    slope = stiffness_slope(pad_rows(solution), stiff_ext, solution)
    gain = intensity_gain(slope, density, intensity, dose_level, clear_level)
    term = jnp.zeros((NX, NY), jnp.float32)
    for kernel in range(K):
        field_re, field_im = fields[kernel]
        back = jnp.stack([field_re * gain, -field_im * gain])
        back_all = jnp.pad(back, ((0, 0), (RADIUS, RADIUS), (RADIUS, RADIUS)))
        col_re, col_im = convolve(back_all[0], back_all[1], tap_table[2, kernel], tap_table[3, kernel], 1, RADIUS, False)
        out_re, out_im = convolve(col_re, col_im, tap_table[0, kernel], tap_table[1, kernel], 0, RADIUS, False)
        term = term + 2.0 * weights[kernel] * out_re
    return term


def reference(design, corner_set, corner_dose, kernel_taps, kernel_weights, support_mask, load_mask, force):
    def accumulate(carry, inputs):
        set_id, dose_level = inputs
        term = one_corner(design, set_id.astype(jnp.int32), dose_level, kernel_taps, kernel_weights, support_mask, load_mask, force)
        return carry + term, None

    total_sum, unused = lax.scan(accumulate, jnp.zeros((NX, NY), jnp.float32), (corner_set, corner_dose))
    return total_sum
```

```python
import functools

import jax
import jax.numpy as jnp
from jax import lax
from jax.experimental import pallas as pl
from jax.experimental.pallas import tpu as pltpu
from jax.sharding import PartitionSpec as P

MESH = pl.DeviceIdType.MESH
LANES = 128
HALO = 24
MASK_HALO = 16
EDGE = 12
PAD = 8

beta_sharp = 8.0
eta_level = 0.25
stiff_floor = 0.05
kappa_ground = 0.1
shear = 0.35
bf16 = jnp.bfloat16
f32 = jnp.float32


def halves(value):
    high = value.astype(bf16)
    return high, (value - high.astype(f32)).astype(bf16)


def dot(left, right):
    return jnp.dot(left, right, preferred_element_type=f32)


def circulant(row, count, shift):
    turned = pltpu.roll(jnp.broadcast_to(row, (8, LANES)), shift, 1) if shift else row
    return pltpu.roll(
        jnp.broadcast_to(turned[:1], (count, LANES)), 0, 1, stride=1, stride_axis=0
    )


def side_lanes(blocks, at):
    zero = jnp.zeros_like(blocks[0])
    before = blocks[at - 1] if at > 0 else zero
    after = blocks[at + 1] if at + 1 < len(blocks) else zero
    lane = lax.broadcasted_iota(jnp.int32, zero.shape, 1)
    return jnp.where(lane < LANES // 2, after, before)


def kernel(
    n_space, n_corner, kernels, radius,
    set_ref, dose_ref, weight_ref, force_ref, design_ref, taps_ref, support_ref, load_ref,
    out_ref,
    tap_rows, base_plain, base_flip,
    col_hi, col_lo, back_col, row_hi, row_lo, back_row_hi, back_row_lo,
    halo, mask_halo, left_hi, left_lo, mid_hi, mid_lo, fields,
    stiff, ground, face_dn, face_rt, loads, image0, image1, factor, gain,
    total, term, share, shares, landed,
    halo_send, halo_recv, share_send, share_recv, term_send, term_recv,
):
    rows, columns = design_ref.shape
    span = rows + 2 * EDGE
    blocks = columns // LANES
    strips = span // 8
    me_s = lax.axis_index("space")
    me_c = lax.axis_index("corner")

    barrier = pltpu.get_barrier_semaphore()
    for off in range(1, n_space):
        pl.semaphore_signal(
            barrier, inc=1, device_id={"space": lax.rem(me_s + off, n_space)}, device_id_type=MESH
        )
    for off in range(1, n_corner):
        pl.semaphore_signal(
            barrier, inc=1, device_id={"corner": lax.rem(me_c + off, n_corner)}, device_id_type=MESH
        )

    chosen = set_ref[0]
    tap_rows[...] = jnp.zeros_like(tap_rows)
    for part in range(4):
        tap_rows[pl.ds(part * kernels, kernels), pl.ds(0, 2 * radius + 1)] = taps_ref[chosen, part]
    table = tap_rows[...]
    base_plain[...] = pltpu.roll(table, LANES - radius, 1)
    from_lane = lax.broadcasted_iota(jnp.int32, (LANES, LANES), 0)
    to_lane = lax.broadcasted_iota(jnp.int32, (LANES, LANES), 1)
    mirror = ((from_lane + to_lane) % LANES == radius).astype(f32)
    base_flip[...] = jnp.dot(
        table, mirror, preferred_element_type=f32, precision=lax.Precision.HIGHEST
    )
    sums = jnp.sum(table, axis=1, keepdims=True)
    sums = [sums[part * kernels:(part + 1) * kernels] for part in range(4)]
    which = lax.broadcasted_iota(jnp.int32, (kernels, 1), 0)
    weight_col = jnp.zeros((kernels, 1), f32)
    for at in range(kernels):
        weight_col = jnp.where(which == at, weight_ref[chosen, at], weight_col)
    clear = jnp.sum(
        weight_col
        * (sums[0] * sums[0] + sums[1] * sums[1])
        * (sums[2] * sums[2] + sums[3] * sums[3]),
        axis=0, keepdims=True,
    )
    dose = dose_ref[0]

    pl.semaphore_wait(barrier, n_space + n_corner - 2)

    def edge_copies(toward):
        other = lax.rem(me_s + (n_space - 1 if toward == 0 else 1), n_space)
        sent = []
        for which_one, (source, target, width) in enumerate((
            (design_ref, halo, HALO),
            (load_ref, mask_halo.at[0], MASK_HALO),
            (support_ref, mask_halo.at[1], MASK_HALO),
        )):
            begin = 0 if toward == 0 else rows - width
            sent.append(pltpu.make_async_remote_copy(
                src_ref=source.at[pl.ds(begin, width)],
                dst_ref=target.at[pl.ds(toward * width, width)],
                send_sem=halo_send.at[toward, which_one],
                recv_sem=halo_recv.at[toward, which_one],
                device_id={"space": other},
                device_id_type=MESH,
            ))
        return sent

    has_before = me_s > 0
    has_after = me_s < n_space - 1

    @pl.when(has_before)
    def _():
        for copy in edge_copies(0):
            copy.start()

    @pl.when(has_after)
    def _():
        for copy in edge_copies(1):
            copy.start()

    near = jnp.abs(from_lane - to_lane) <= radius
    lane_row = lax.broadcasted_iota(jnp.int32, (span, LANES), 1)
    lane_out = lax.broadcasted_iota(jnp.int32, (rows, LANES), 1)
    reach = rows + 2 * HALO

    def build(at, carry):
        def plain(part):
            return base_plain[pl.ds(part * kernels + at, 1), :]

        def flip(part):
            return base_flip[pl.ds(part * kernels + at, 1), :]

        for part in range(2):
            band = circulant(plain(2 + part), LANES, 0)
            hi, lo = halves(band)
            zero = jnp.zeros_like(hi)
            there = pl.ds(part * LANES, LANES)
            col_hi[at, pl.ds(0, LANES), there] = jnp.where(near, hi, zero)
            col_hi[at, pl.ds(LANES, LANES), there] = jnp.where(near, zero, hi)
            col_lo[at, pl.ds(0, LANES), there] = jnp.where(near, lo, zero)
            col_lo[at, pl.ds(LANES, LANES), there] = jnp.where(near, zero, lo)
            band = circulant(flip(2 + part), LANES, 0)
            hi, lo = halves(band)
            for value, lanes in ((hi, 0), (lo, LANES)):
                back_col[at, pl.ds(2 * part * LANES, LANES), pl.ds(lanes, LANES)] = jnp.where(near, value, zero)
                back_col[at, pl.ds((2 * part + 1) * LANES, LANES), pl.ds(lanes, LANES)] = jnp.where(near, zero, value)

        def joined(first, second, lane, width):
            turned = pltpu.roll(second, width, 1)
            left = jnp.where(lane < width, first, turned)
            right = jnp.where(lane < 2 * width - LANES, turned, 0.0)
            return jnp.concatenate([left, right], axis=1)

        def forward_rows(part):
            band = circulant(flip(part), span, LANES - EDGE)
            band = jnp.where(lane_row < rows + HALO, band, pltpu.roll(band, reach, 1))
            return jnp.where(lane_row < reach, band, 0.0)

        row_re = forward_rows(0)
        row_im = forward_rows(1)
        matrix = jnp.concatenate(
            [joined(row_re, -row_im, lane_row, reach), joined(row_im, row_re, lane_row, reach)], axis=0
        )
        hi, lo = halves(matrix)
        row_hi[at] = hi
        row_lo[at] = lo
        scale = 2.0 * weight_ref[chosen, at]
        row_re = circulant(plain(0), rows, EDGE) * scale
        row_im = circulant(plain(1), rows, EDGE) * scale
        matrix = jnp.concatenate(
            [joined(row_re, -row_im, lane_out, span), joined(-row_im, -row_re, lane_out, span)], axis=0
        )
        hi, lo = halves(matrix)
        back_row_hi[at] = hi
        back_row_lo[at] = lo
        return carry

    lax.fori_loop(0, kernels, build, 0)

    def columns_of(cells, begin):
        parts = [cells[:, at * LANES:(at + 1) * LANES] for at in range(blocks)]
        for at in range(blocks):
            whole = jnp.concatenate([parts[at], side_lanes(parts, at)], axis=1)
            hi, lo = halves(whole)
            left_hi[pl.ds(at * rows, rows), :] = hi
            left_lo[pl.ds(at * rows, rows), :] = lo

        def one(at, carry):
            value = (
                dot(left_hi[...], col_hi[at])
                + dot(left_hi[...], col_lo[at])
                + dot(left_lo[...], col_hi[at])
            )
            hi, lo = halves(value)
            for block in range(blocks):
                for part in range(2):
                    here = (slice(block * rows, (block + 1) * rows), slice(part * LANES, (part + 1) * LANES))
                    there = (at, pl.ds(part * reach + begin, rows), pl.ds(block * LANES, LANES))
                    mid_hi[there] = hi[here]
                    mid_lo[there] = lo[here]
            return carry

        lax.fori_loop(0, kernels, one, 0)

    columns_of(design_ref[...], 0)

    @pl.when(has_after)
    def _():
        for copy in edge_copies(0):
            copy.wait_recv()

    @pl.when(jnp.logical_not(has_after))
    def _():
        halo[pl.ds(0, HALO), :] = jnp.zeros((HALO, columns), f32)
        mask_halo[:, pl.ds(0, MASK_HALO), :] = jnp.zeros((2, MASK_HALO, columns), jnp.int32)

    @pl.when(has_before)
    def _():
        for copy in edge_copies(1):
            copy.wait_recv()

    @pl.when(jnp.logical_not(has_before))
    def _():
        halo[pl.ds(HALO, HALO), :] = jnp.zeros((HALO, columns), f32)
        mask_halo[:, pl.ds(MASK_HALO, MASK_HALO), :] = jnp.zeros((2, MASK_HALO, columns), jnp.int32)

    columns_of(halo[...], rows)

    def rows_of(at, carry):
        fields[at] = (
            dot(row_hi[at][:, :2 * reach], mid_hi[at])
            + dot(row_hi[at][:, :2 * reach], mid_lo[at])
            + dot(row_lo[at][:, :2 * reach], mid_hi[at])
        )
        return carry

    lax.fori_loop(0, kernels, rows_of, 0)

    zero_pad = jnp.zeros((PAD, columns), f32)
    for array in (stiff, face_dn, loads, image0, image1):
        array[pl.ds(0, PAD), :] = zero_pad
        array[pl.ds(PAD + span, PAD), :] = zero_pad
    for which_one, own, target, base in ((0, load_ref, loads, PAD), (1, support_ref, ground, 0)):
        target[pl.ds(base, EDGE), :] = mask_halo[which_one, pl.ds(2 * MASK_HALO - EDGE, EDGE), :].astype(f32)
        target[pl.ds(base + EDGE, rows), :] = own[...].astype(f32)
        target[pl.ds(base + EDGE + rows, EDGE), :] = mask_halo[which_one, pl.ds(0, EDGE), :].astype(f32)

    row_in = lax.broadcasted_iota(jnp.int32, (8, columns), 0)
    lane_in = lax.broadcasted_iota(jnp.int32, (8, columns), 1)
    first_row = me_s * rows - EDGE
    grid_rows = n_space * rows
    spread = jnp.tanh(beta_sharp * eta_level) + jnp.tanh(beta_sharp * (1.0 - eta_level))
    low_end = jnp.tanh(beta_sharp * eta_level)
    weights = [weight_ref[chosen, at] for at in range(kernels)]
    gain_scale = dose * (3.0 * (1.0 - stiff_floor) * beta_sharp) / (clear * spread)

    def strip_of(strip):
        return pl.multiple_of(strip * 8, 8)

    def row_above(array, begin, here):
        before = array[pl.ds(begin + PAD - 8, 8), :]
        return jnp.where(row_in == 0, pltpu.roll(before, 1, 0), pltpu.roll(here, 1, 0))

    def row_below(array, begin, here):
        after = array[pl.ds(begin + PAD + 8, 8), :]
        return jnp.where(row_in == 7, pltpu.roll(after, 7, 0), pltpu.roll(here, 7, 0))

    def project(strip, carry):
        begin = strip_of(strip)
        bright = jnp.zeros((8, columns), f32)
        for at in range(kernels):
            re = fields[at, pl.ds(begin, 8), :]
            im = fields[at, pl.ds(span + begin, 8), :]
            bright = bright + weights[at] * (re * re + im * im)
        bright = dose * bright / clear
        bent = jnp.tanh(beta_sharp * (bright - eta_level))
        density = (low_end + bent) / spread
        square = density * density
        grid_row = row_in + (first_row + begin)
        inside = (grid_row >= 0) & (grid_row < grid_rows)
        hard = jnp.where(inside, stiff_floor + (1.0 - stiff_floor) * square * density, 0.0)
        stiff[pl.ds(begin + PAD, 8), :] = hard
        ground[pl.ds(begin, 8), :] = kappa_ground * hard + ground[pl.ds(begin, 8), :]
        factor[pl.ds(begin, 8), :] = jnp.where(
            inside, -gain_scale * square * (1.0 - bent * bent), 0.0
        )
        return carry

    lax.fori_loop(0, strips, project, 0)

    def faces(strip, carry):
        begin = strip_of(strip)
        here = stiff[pl.ds(begin + PAD, 8), :]
        below = row_below(stiff, begin, here)
        face_dn[pl.ds(begin + PAD, 8), :] = 2.0 * here * below / jnp.maximum(here + below, 1e-20)
        right = pltpu.roll(here, columns - 1, 1)
        face = 2.0 * here * right / jnp.maximum(here + right, 1e-20)
        face_rt[pl.ds(begin, 8), :] = jnp.where(lane_in < columns - 1, face, 0.0)
        return carry

    lax.fori_loop(0, strips, faces, 0)

    force0 = force_ref[0]
    force1 = force_ref[1]

    def around(strip):
        begin = strip_of(strip)
        right = face_rt[pl.ds(begin, 8), :]
        down = face_dn[pl.ds(begin + PAD, 8), :]
        return row_above(face_dn, begin, down), down, pltpu.roll(right, 1, 1), right

    def three(array, strip):
        begin = strip_of(strip)
        here = array[pl.ds(begin + PAD, 8), :]
        return row_above(array, begin, here), here, row_below(array, begin, here)

    def own_rows(strip):
        row = row_in + strip_of(strip)
        return (row >= EDGE) & (row < EDGE + rows)

    def flows(above, here, below, sides):
        face_up, face_down, face_left, face_right = sides
        along_rows = face_up * (here - above) + face_down * (here - below)
        along_columns = face_left * (here - pltpu.roll(here, 1, 1)) + face_right * (
            here - pltpu.roll(here, columns - 1, 1)
        )
        return along_rows, along_columns

    def first_image(strip, carry):
        norm, energy = carry
        begin = strip_of(strip)
        above, here, below = three(loads, strip)
        along_rows, along_columns = flows(above, here, below, around(strip))
        held = ground[pl.ds(begin, 8), :] * here
        one = force0 * (held + along_rows + shear * along_columns)
        two = force1 * (held + shear * along_rows + along_columns)
        image0[pl.ds(begin + PAD, 8), :] = one
        image1[pl.ds(begin + PAD, 8), :] = two
        own = jnp.where(own_rows(strip), here, 0.0)
        return norm + own * own, energy + own * (force0 * one + force1 * two)

    blank = jnp.zeros((8, columns), f32)
    norm, energy = lax.fori_loop(0, strips, first_image, (blank, blank))

    def whole_sum(cells):
        return jnp.sum(jnp.sum(cells, axis=0, keepdims=True), axis=1, keepdims=True)

    norm = whole_sum(norm) * (force0 * force0 + force1 * force1)
    energy = whole_sum(energy)
    ratio = jnp.where(norm > 0.0, energy / jnp.where(norm > 0.0, norm, 1.0), 0.0)

    def second_image(strip, carry):
        sums = list(carry)
        sides = around(strip)
        load3 = three(loads, strip)
        held = ground[pl.ds(strip_of(strip), 8), :]
        keep = own_rows(strip)
        for array, push, of_rows, of_columns in (
            (image0, force0, 1.0, shear), (image1, force1, shear, 1.0)
        ):
            image3 = three(array, strip)
            lean = ratio * push
            above, here, below = [image3[at] - lean * load3[at] for at in range(3)]
            along_rows, along_columns = flows(above, here, below, sides)
            applied = held * here + of_rows * along_rows + of_columns * along_columns
            applied = jnp.where(keep, applied, 0.0)
            sums[0] = sums[0] + jnp.where(keep, here * here, 0.0)
            sums[1] = sums[1] + here * applied
            sums[2] = sums[2] + push * load3[1] * applied
        return tuple(sums)

    first_strip = EDGE // 8
    last_strip = (EDGE + rows + 7) // 8
    rest = lax.fori_loop(first_strip, last_strip, second_image, (blank, blank, blank))
    values = [norm, ratio] + [whole_sum(cells) for cells in rest]
    lane8 = lax.broadcasted_iota(jnp.int32, (8, LANES), 1)
    packed = jnp.zeros((8, LANES), f32)
    for at, value in enumerate(values):
        packed = jnp.where(lane8 == at, value, packed)
    share[...] = packed

    def share_copy(off):
        return pltpu.make_async_remote_copy(
            src_ref=share,
            dst_ref=shares.at[off - 1],
            send_sem=share_send.at[off - 1],
            recv_sem=share_recv.at[off - 1],
            device_id={"space": lax.rem(me_s + off, n_space)},
            device_id_type=MESH,
        )

    for off in range(1, n_space):
        share_copy(off).start()
    for off in range(1, n_space):
        share_copy(off).wait_recv()
    tables = [packed] + [shares[off - 1] for off in range(1, n_space)]
    lists = [[each[0:1, at:at + 1] for at in range(5)] for each in tables]
    norm_now = sum(each[0] for each in lists)
    centre = sum(each[0] * each[1] for each in lists) / norm_now
    spare = 0.0
    bend = 0.0
    for part_norm, part_ratio, part_spare, part_bend, part_cross in lists:
        shift = part_ratio - centre
        spare = spare + part_spare + shift * shift * part_norm
        bend = bend + part_bend + shift * (part_cross + part_spare) + shift * shift * part_ratio * part_norm
    inverse = 1.0 / centre
    norm_next = spare * inverse * inverse
    renew = norm_next / norm_now
    curve = bend * inverse * inverse - renew * norm_next * centre
    step = norm_next / curve
    of_load = inverse + step * (1.0 + renew)
    of_image = -step * inverse

    def slopes(strip, carry):
        begin = strip_of(strip)
        sides = around(strip)
        squares = [side * side for side in sides]
        load3 = three(loads, strip)
        here_stiff = stiff[pl.ds(begin + PAD, 8), :]
        held = jnp.zeros((8, columns), f32)
        bent = jnp.zeros((8, columns), f32)
        for array, push, of_rows, of_columns in (
            (image0, force0, 1.0, shear), (image1, force1, shear, 1.0)
        ):
            image3 = three(array, strip)
            above, here, below = [
                (of_load * push) * load3[at] + of_image * image3[at] for at in range(3)
            ]
            up = here - above
            down = here - below
            left = here - pltpu.roll(here, 1, 1)
            right = here - pltpu.roll(here, columns - 1, 1)
            held = held + here * here
            bent = (
                bent
                + of_rows * (squares[0] * (up * up) + squares[1] * (down * down))
                + of_columns * (squares[2] * (left * left) + squares[3] * (right * right))
            )
        bent = bent * 0.5 / jnp.maximum(here_stiff * here_stiff, 1e-6)
        gain[pl.ds(begin, 8), :] = factor[pl.ds(begin, 8), :] * (kappa_ground * held + bent)
        return carry

    lax.fori_loop(0, strips, slopes, 0)

    total[...] = jnp.zeros_like(total)

    def back(at, carry):
        scale = gain[...]
        sent = jnp.concatenate(
            [fields[at, pl.ds(0, span), :] * scale, -(fields[at, pl.ds(span, span), :] * scale)], axis=0
        )
        hi, lo = halves(sent)
        turned = (
            dot(back_row_hi[at][:, :2 * span], hi)
            + dot(back_row_hi[at][:, :2 * span], lo)
            + dot(back_row_lo[at][:, :2 * span], hi)
        )
        grids = []
        for part in range(2):
            piece = turned[part * rows:(part + 1) * rows]
            parts = [piece[:, block * LANES:(block + 1) * LANES] for block in range(blocks)]
            grids.append([
                jnp.concatenate([parts[block], side_lanes(parts, block)], axis=1)
                for block in range(blocks)
            ])
        whole = jnp.concatenate(
            [jnp.concatenate([grids[0][block], grids[1][block]], axis=1) for block in range(blocks)], axis=0
        )
        hi, lo = halves(whole)
        wide = dot(hi, back_col[at])
        total[...] += wide[:, :LANES] + wide[:, LANES:] + dot(lo, back_col[at][:, :LANES])
        return carry

    lax.fori_loop(0, kernels, back, 0)
    for block in range(blocks):
        term[block] = total[pl.ds(block * rows, rows), :]

    width = columns // n_corner
    per_block = LANES // width

    def term_copy(off):
        other = lax.rem(me_c + off, n_corner)
        return pltpu.make_async_remote_copy(
            src_ref=term.at[other // per_block],
            dst_ref=landed.at[off - 1],
            send_sem=term_send.at[off - 1],
            recv_sem=term_recv.at[off - 1],
            device_id={"corner": other},
            device_id_type=MESH,
        )

    for off in range(1, n_corner):
        term_copy(off).start()
    summed = term[me_c // per_block]
    for off in range(1, n_corner):
        term_copy(off).wait_recv()
        summed = summed + landed[off - 1]
    if per_block == 1:
        out_ref[...] = summed
    else:
        place = lax.rem(me_c, per_block)
        kept = jnp.zeros(out_ref.shape, f32)
        for at in range(per_block):
            kept = kept + jnp.where(place == at, 1.0, 0.0) * summed[:, at * width:(at + 1) * width]
        out_ref[...] = kept

    for off in range(1, n_corner):
        term_copy(off).wait_send()
    for off in range(1, n_space):
        share_copy(off).wait_send()

    @pl.when(has_before)
    def _():
        for copy in edge_copies(0):
            copy.wait_send()

    @pl.when(has_after)
    def _():
        for copy in edge_copies(1):
            copy.wait_send()


def on_device(
    n_space, n_corner,
    design, corner_set, corner_dose, kernel_taps, kernel_weights, support_mask, load_mask, force,
):
    rows, columns = design.shape
    kernels = kernel_taps.shape[2]
    radius = kernel_taps.shape[3] // 2
    span = rows + 2 * EDGE
    reach = rows + 2 * HALO
    blocks = columns // LANES
    padded_rows = span + 2 * PAD
    in_smem = pl.BlockSpec(memory_space=pltpu.SMEM)
    in_vmem = pl.BlockSpec(memory_space=pltpu.VMEM)
    scratch = [
        pltpu.VMEM((4 * kernels, LANES), f32),
        pltpu.VMEM((4 * kernels, LANES), f32),
        pltpu.VMEM((4 * kernels, LANES), f32),
        pltpu.VMEM((kernels, 2 * LANES, 2 * LANES), bf16),
        pltpu.VMEM((kernels, 2 * LANES, 2 * LANES), bf16),
        pltpu.VMEM((kernels, 4 * LANES, 2 * LANES), bf16),
        pltpu.VMEM((kernels, 2 * span, 2 * LANES), bf16),
        pltpu.VMEM((kernels, 2 * span, 2 * LANES), bf16),
        pltpu.VMEM((kernels, 2 * rows, 2 * LANES), bf16),
        pltpu.VMEM((kernels, 2 * rows, 2 * LANES), bf16),
        pltpu.VMEM((2 * HALO, columns), f32),
        pltpu.VMEM((2, 2 * MASK_HALO, columns), jnp.int32),
        pltpu.VMEM((blocks * rows, 2 * LANES), bf16),
        pltpu.VMEM((blocks * rows, 2 * LANES), bf16),
        pltpu.VMEM((kernels, 2 * reach, columns), bf16),
        pltpu.VMEM((kernels, 2 * reach, columns), bf16),
        pltpu.VMEM((kernels, 2 * span, columns), f32),
        pltpu.VMEM((padded_rows, columns), f32),
        pltpu.VMEM((span, columns), f32),
        pltpu.VMEM((padded_rows, columns), f32),
        pltpu.VMEM((span, columns), f32),
        pltpu.VMEM((padded_rows, columns), f32),
        pltpu.VMEM((padded_rows, columns), f32),
        pltpu.VMEM((padded_rows, columns), f32),
        pltpu.VMEM((span, columns), f32),
        pltpu.VMEM((span, columns), f32),
        pltpu.VMEM((blocks * rows, LANES), f32),
        pltpu.VMEM((blocks, rows, LANES), f32),
        pltpu.VMEM((8, LANES), f32),
        pltpu.VMEM((n_space - 1, 8, LANES), f32),
        pltpu.VMEM((n_corner - 1, rows, LANES), f32),
        pltpu.SemaphoreType.DMA((2, 3)),
        pltpu.SemaphoreType.DMA((2, 3)),
        pltpu.SemaphoreType.DMA((n_space - 1,)),
        pltpu.SemaphoreType.DMA((n_space - 1,)),
        pltpu.SemaphoreType.DMA((n_corner - 1,)),
        pltpu.SemaphoreType.DMA((n_corner - 1,)),
    ]
    return pl.pallas_call(
        functools.partial(kernel, n_space, n_corner, kernels, radius),
        out_shape=jax.ShapeDtypeStruct((rows, columns // n_corner), f32),
        in_specs=[in_smem] * 4 + [in_vmem] * 4,
        out_specs=in_vmem,
        scratch_shapes=scratch,
        compiler_params=pltpu.CompilerParams(
            collective_id=0, has_side_effects=True, vmem_limit_bytes=48 * 1024 * 1024
        ),
    )(
        corner_set, corner_dose, kernel_weights, force,
        design, kernel_taps, support_mask, load_mask,
    )


def solution(mesh):
    placed = (
        P("space", None),
        P("corner"),
        P("corner"),
        P(),
        P(),
        P("space", None),
        P("space", None),
        P(),
    )
    body = functools.partial(on_device, mesh.shape["space"], mesh.shape["corner"])
    return jax.shard_map(
        body, mesh=mesh, in_specs=placed, out_specs=P("space", "corner"), check_vma=False
    )
```

```python
import functools
import math

import jax
import jax.numpy as jnp
from jax import lax
from jax.experimental import pallas as pl
from jax.experimental.pallas import tpu as pltpu
from jax.sharding import PartitionSpec as P

MESH = pl.DeviceIdType.MESH
LANES = 128
HALO = 24
MASK_HALO = 16
EDGE = 12
PAD = 8

beta_sharp = 8.0
eta_level = 0.25
stiff_floor = 0.05
kappa_ground = 0.1
shear = 0.35
bf16 = jnp.bfloat16
f32 = jnp.float32


def halves(value):
    high = value.astype(bf16)
    return high, (value - high.astype(f32)).astype(bf16)


def dot(left, right):
    return jnp.dot(left, right, preferred_element_type=f32)


def circulant(row, count, shift):
    turned = pltpu.roll(jnp.broadcast_to(row, (8, LANES)), shift, 1) if shift else row
    return pltpu.roll(
        jnp.broadcast_to(turned[:1], (count, LANES)), 0, 1, stride=1, stride_axis=0
    )


def side_lanes(blocks, at):
    zero = jnp.zeros_like(blocks[0])
    before = blocks[at - 1] if at > 0 else zero
    after = blocks[at + 1] if at + 1 < len(blocks) else zero
    lane = lax.broadcasted_iota(jnp.int32, zero.shape, 1)
    return jnp.where(lane < LANES // 2, after, before)


def kernel(
    n_space, n_corner, kernels, radius,
    set_any, dose_any, weight_any, force_any, design_any, taps_any, support_any, load_any,
    out_ref,
    set_ref, dose_ref, weight_ref, force_ref, design_ref, taps_ref, support_ref, load_ref,
    tap_rows, base_plain, base_flip,
    col_all, back_col, row_both, back_row_both,
    halo, mask_halo, left_all, mid_hi, mid_lo, fields, back_hi, back_lo,
    stiff, ground, face_dn, face_rt, loads, image0, image1, factor, gain,
    term, share, shares, landed,
    local_sem, halo_send, halo_recv, share_send, share_recv, term_send, term_recv,
):
    local = [
        pltpu.make_async_copy(source, target, local_sem.at[at])
        for at, (source, target) in enumerate((
            (taps_any, taps_ref), (set_any, set_ref), (dose_any, dose_ref), (weight_any, weight_ref),
            (force_any, force_ref), (design_any, design_ref), (load_any, load_ref), (support_any, support_ref),
        ))
    ]
    for copy in local:
        copy.start()
    rows, columns = design_ref.shape
    span = rows + 2 * EDGE
    blocks = columns // LANES
    strips = span // 8
    me_s = lax.axis_index("space")
    me_c = lax.axis_index("corner")

    barrier = pltpu.get_barrier_semaphore()
    for off in range(1, n_space):
        pl.semaphore_signal(
            barrier, inc=1, device_id={"space": lax.rem(me_s + off, n_space)}, device_id_type=MESH
        )
    for off in range(1, n_corner):
        pl.semaphore_signal(
            barrier, inc=1, device_id={"corner": lax.rem(me_c + off, n_corner)}, device_id_type=MESH
        )

    pl.semaphore_wait(barrier, n_space + n_corner - 2)

    def edge_copies(toward):
        other = lax.rem(me_s + (n_space - 1 if toward == 0 else 1), n_space)
        sent = []
        for which_one, (source, target, width) in enumerate((
            (design_any, halo, HALO),
            (load_any, mask_halo.at[0], MASK_HALO),
            (support_any, mask_halo.at[1], MASK_HALO),
        )):
            begin = 0 if toward == 0 else rows - width
            sent.append(pltpu.make_async_remote_copy(
                src_ref=source.at[pl.ds(begin, width)],
                dst_ref=target.at[pl.ds(toward * width, width)],
                send_sem=halo_send.at[toward, which_one],
                recv_sem=halo_recv.at[toward, which_one],
                device_id={"space": other},
                device_id_type=MESH,
            ))
        return sent

    has_before = me_s > 0
    has_after = me_s < n_space - 1

    @pl.when(has_before)
    def _():
        for copy in edge_copies(0):
            copy.start()

    @pl.when(has_after)
    def _():
        for copy in edge_copies(1):
            copy.start()

    for copy in local[:5]:
        copy.wait()

    chosen = set_ref[0]
    tap_rows[...] = jnp.zeros_like(tap_rows)
    for part in range(4):
        tap_rows[pl.ds(part * kernels, kernels), pl.ds(0, 2 * radius + 1)] = taps_ref[chosen, part]
    table = tap_rows[...]
    base_plain[...] = pltpu.roll(table, LANES - radius, 1)
    from_lane = lax.broadcasted_iota(jnp.int32, (LANES, LANES), 0)
    to_lane = lax.broadcasted_iota(jnp.int32, (LANES, LANES), 1)
    mirror = ((from_lane + to_lane) % LANES == radius).astype(f32)
    base_flip[...] = jnp.dot(
        table, mirror, preferred_element_type=f32, precision=lax.Precision.HIGHEST
    )
    sums = jnp.sum(table, axis=1, keepdims=True)
    sums = [sums[part * kernels:(part + 1) * kernels] for part in range(4)]
    which = lax.broadcasted_iota(jnp.int32, (kernels, 1), 0)
    weight_col = jnp.zeros((kernels, 1), f32)
    for at in range(kernels):
        weight_col = jnp.where(which == at, weight_ref[chosen, at], weight_col)
    clear = jnp.sum(
        weight_col
        * (sums[0] * sums[0] + sums[1] * sums[1])
        * (sums[2] * sums[2] + sums[3] * sums[3]),
        axis=0, keepdims=True,
    )
    dose = dose_ref[0]

    near = jnp.abs(from_lane - to_lane) <= radius
    lane_row = lax.broadcasted_iota(jnp.int32, (span, LANES), 1)
    lane_out = lax.broadcasted_iota(jnp.int32, (rows, LANES), 1)
    reach = rows + 2 * HALO

    def build(at, carry):
        def plain(part):
            return base_plain[pl.ds(part * kernels + at, 1), :]

        def flip(part):
            return base_flip[pl.ds(part * kernels + at, 1), :]

        for part in range(2):
            band = circulant(plain(2 + part), LANES, 0)
            hi, lo = halves(band)
            zero = jnp.zeros_like(hi)
            there = pl.ds(part * LANES, LANES)
            for place, value in ((0, hi), (1, lo), (2, hi)):
                col_all[at, pl.ds(2 * place * LANES, LANES), there] = jnp.where(near, value, zero)
                col_all[at, pl.ds((2 * place + 1) * LANES, LANES), there] = jnp.where(near, zero, value)
            band = circulant(flip(2 + part), LANES, 0)
            hi, lo = halves(band)
            for value, lanes in ((hi, 0), (lo, LANES)):
                place = pl.multiple_of(at * (4 * LANES), LANES) + 2 * part * LANES
                back_col[pl.ds(place, LANES), pl.ds(lanes, LANES)] = jnp.where(near, value, zero)
                back_col[pl.ds(place + LANES, LANES), pl.ds(lanes, LANES)] = jnp.where(near, zero, value)

        def joined(first, second, lane, width):
            turned = pltpu.roll(second, width, 1)
            left = jnp.where(lane < width, first, turned)
            right = jnp.where(lane < 2 * width - LANES, turned, 0.0)
            return jnp.concatenate([left, right], axis=1)

        def forward_rows(part):
            band = circulant(flip(part), span, LANES - EDGE)
            band = jnp.where(lane_row < rows + HALO, band, pltpu.roll(band, reach, 1))
            return jnp.where(lane_row < reach, band, 0.0)

        row_re = forward_rows(0)
        row_im = forward_rows(1)
        matrix = jnp.concatenate(
            [joined(row_re, -row_im, lane_row, reach), joined(row_im, row_re, lane_row, reach)], axis=0
        )
        hi, lo = halves(matrix)
        row_both[at, pl.ds(0, 2 * span), :] = hi
        row_both[at, pl.ds(2 * span, 2 * span), :] = lo
        scale = 2.0 * weight_ref[chosen, at]
        row_re = circulant(plain(0), rows, EDGE) * scale
        row_im = circulant(plain(1), rows, EDGE) * scale
        matrix = jnp.concatenate(
            [joined(row_re, -row_im, lane_out, span), joined(-row_im, -row_re, lane_out, span)], axis=0
        )
        hi, lo = halves(matrix)
        back_row_both[at, pl.ds(0, 2 * rows), :] = hi
        back_row_both[at, pl.ds(2 * rows, 2 * rows), :] = lo
        return carry

    lax.fori_loop(0, kernels, build, 0)

    def columns_of(cells, begin):
        parts = [cells[:, at * LANES:(at + 1) * LANES] for at in range(blocks)]
        for at in range(blocks):
            whole = jnp.concatenate([parts[at], side_lanes(parts, at)], axis=1)
            hi, lo = halves(whole)
            left_all[pl.ds(at * rows, rows), :] = jnp.concatenate([hi, hi, lo], axis=1)

        for at in range(kernels):
            value = dot(left_all[...], col_all[at])
            hi, lo = halves(value)
            for block in range(blocks):
                for part in range(2):
                    here = (slice(block * rows, (block + 1) * rows), slice(part * LANES, (part + 1) * LANES))
                    there = (at, pl.ds(part * reach + begin, rows), pl.ds(block * LANES, LANES))
                    mid_hi[there] = hi[here]
                    mid_lo[there] = lo[here]

    local[5].wait()
    columns_of(design_ref[...], 0)

    @pl.when(has_after)
    def _():
        for copy in edge_copies(0):
            copy.wait_recv()

    @pl.when(jnp.logical_not(has_after))
    def _():
        halo[pl.ds(0, HALO), :] = jnp.zeros((HALO, columns), f32)
        mask_halo[:, pl.ds(0, MASK_HALO), :] = jnp.zeros((2, MASK_HALO, columns), jnp.int32)

    @pl.when(has_before)
    def _():
        for copy in edge_copies(1):
            copy.wait_recv()

    @pl.when(jnp.logical_not(has_before))
    def _():
        halo[pl.ds(HALO, HALO), :] = jnp.zeros((HALO, columns), f32)
        mask_halo[:, pl.ds(MASK_HALO, MASK_HALO), :] = jnp.zeros((2, MASK_HALO, columns), jnp.int32)

    columns_of(halo[...], rows)

    for at in range(kernels):
        both = row_both[at][:, :2 * reach]
        of_high = dot(both, mid_hi[at])
        fields[at] = of_high[:2 * span] + of_high[2 * span:] + dot(both[:2 * span], mid_lo[at])

    for copy in local[6:]:
        copy.wait()

    zero_pad = jnp.zeros((PAD, columns), f32)
    for array in (stiff, face_dn, loads, image0, image1):
        array[pl.ds(0, PAD), :] = zero_pad
        array[pl.ds(PAD + span, PAD), :] = zero_pad
    for which_one, own, target, base in ((0, load_ref, loads, PAD), (1, support_ref, ground, 0)):
        target[pl.ds(base, EDGE), :] = mask_halo[which_one, pl.ds(2 * MASK_HALO - EDGE, EDGE), :].astype(f32)
        target[pl.ds(base + EDGE, rows), :] = own[...].astype(f32)
        target[pl.ds(base + EDGE + rows, EDGE), :] = mask_halo[which_one, pl.ds(0, EDGE), :].astype(f32)

    row_in = lax.broadcasted_iota(jnp.int32, (8, columns), 0)
    lane_in = lax.broadcasted_iota(jnp.int32, (8, columns), 1)
    first_row = me_s * rows - EDGE
    grid_rows = n_space * rows
    low_end = math.tanh(beta_sharp * eta_level)
    spread = low_end + math.tanh(beta_sharp * (1.0 - eta_level))
    weights = [weight_ref[chosen, at] for at in range(kernels)]
    level = dose / clear
    gain_scale = level * (3.0 * (1.0 - stiff_floor) * beta_sharp / spread)

    def strip_of(strip):
        return pl.multiple_of(strip * 8, 8)

    def row_above(array, begin, here):
        before = array[pl.ds(begin + PAD - 8, 8), :]
        return jnp.where(row_in == 0, pltpu.roll(before, 1, 0), pltpu.roll(here, 1, 0))

    def row_below(array, begin, here):
        after = array[pl.ds(begin + PAD + 8, 8), :]
        return jnp.where(row_in == 7, pltpu.roll(after, 7, 0), pltpu.roll(here, 7, 0))

    def project(strip, carry):
        begin = strip_of(strip)
        bright = jnp.zeros((8, columns), f32)
        for at in range(kernels):
            re = fields[at, pl.ds(begin, 8), :]
            im = fields[at, pl.ds(span + begin, 8), :]
            bright = bright + weights[at] * (re * re + im * im)
        bright = bright * level
        bent = jnp.tanh(beta_sharp * (bright - eta_level))
        density = (low_end + bent) * (1.0 / spread)
        square = density * density
        grid_row = row_in + (first_row + begin)
        inside = (grid_row >= 0) & (grid_row < grid_rows)
        hard = jnp.where(inside, stiff_floor + (1.0 - stiff_floor) * square * density, 0.0)
        stiff[pl.ds(begin + PAD, 8), :] = hard
        ground[pl.ds(begin, 8), :] = kappa_ground * hard + ground[pl.ds(begin, 8), :]
        factor[pl.ds(begin, 8), :] = jnp.where(
            inside, -gain_scale * square * (1.0 - bent * bent), 0.0
        )
        return carry

    lax.fori_loop(0, strips, project, 0)

    def faces(strip, carry):
        begin = strip_of(strip)
        here = stiff[pl.ds(begin + PAD, 8), :]
        below = row_below(stiff, begin, here)
        face_dn[pl.ds(begin + PAD, 8), :] = 2.0 * here * below / jnp.maximum(here + below, 1e-20)
        right = pltpu.roll(here, columns - 1, 1)
        face = 2.0 * here * right / jnp.maximum(here + right, 1e-20)
        face_rt[pl.ds(begin, 8), :] = jnp.where(lane_in < columns - 1, face, 0.0)
        return carry

    lax.fori_loop(0, strips, faces, 0)

    force0 = force_ref[0]
    force1 = force_ref[1]

    def around(strip):
        begin = strip_of(strip)
        right = face_rt[pl.ds(begin, 8), :]
        down = face_dn[pl.ds(begin + PAD, 8), :]
        return row_above(face_dn, begin, down), down, pltpu.roll(right, 1, 1), right

    def three(array, strip):
        begin = strip_of(strip)
        here = array[pl.ds(begin + PAD, 8), :]
        return row_above(array, begin, here), here, row_below(array, begin, here)

    def own_rows(strip):
        row = row_in + strip_of(strip)
        return (row >= EDGE) & (row < EDGE + rows)

    def flows(above, here, below, sides):
        face_up, face_down, face_left, face_right = sides
        along_rows = face_up * (here - above) + face_down * (here - below)
        along_columns = face_left * (here - pltpu.roll(here, 1, 1)) + face_right * (
            here - pltpu.roll(here, columns - 1, 1)
        )
        return along_rows, along_columns

    def first_image(strip, carry):
        norm, energy = carry
        begin = strip_of(strip)
        above, here, below = three(loads, strip)
        along_rows, along_columns = flows(above, here, below, around(strip))
        held = ground[pl.ds(begin, 8), :] * here
        one = force0 * (held + along_rows + shear * along_columns)
        two = force1 * (held + shear * along_rows + along_columns)
        image0[pl.ds(begin + PAD, 8), :] = one
        image1[pl.ds(begin + PAD, 8), :] = two
        own = jnp.where(own_rows(strip), here, 0.0)
        return norm + own * own, energy + own * (force0 * one + force1 * two)

    blank = jnp.zeros((8, columns), f32)
    norm, energy = lax.fori_loop(0, strips, first_image, (blank, blank))

    def whole_sum(cells):
        return jnp.sum(jnp.sum(cells, axis=0, keepdims=True), axis=1, keepdims=True)

    norm = whole_sum(norm) * (force0 * force0 + force1 * force1)
    energy = whole_sum(energy)
    ratio = jnp.where(norm > 0.0, energy / jnp.where(norm > 0.0, norm, 1.0), 0.0)

    def second_image(strip, carry):
        sums = list(carry)
        sides = around(strip)
        load3 = three(loads, strip)
        held = ground[pl.ds(strip_of(strip), 8), :]
        keep = own_rows(strip)
        for array, push, of_rows, of_columns in (
            (image0, force0, 1.0, shear), (image1, force1, shear, 1.0)
        ):
            image3 = three(array, strip)
            lean = ratio * push
            above, here, below = [image3[at] - lean * load3[at] for at in range(3)]
            along_rows, along_columns = flows(above, here, below, sides)
            applied = held * here + of_rows * along_rows + of_columns * along_columns
            applied = jnp.where(keep, applied, 0.0)
            sums[0] = sums[0] + jnp.where(keep, here * here, 0.0)
            sums[1] = sums[1] + here * applied
            sums[2] = sums[2] + push * load3[1] * applied
        return tuple(sums)

    first_strip = EDGE // 8
    last_strip = (EDGE + rows + 7) // 8
    rest = lax.fori_loop(first_strip, last_strip, second_image, (blank, blank, blank))
    values = [norm, ratio] + [whole_sum(cells) for cells in rest]
    lane8 = lax.broadcasted_iota(jnp.int32, (8, LANES), 1)
    packed = jnp.zeros((8, LANES), f32)
    for at, value in enumerate(values):
        packed = jnp.where(lane8 == at, value, packed)
    share[...] = packed

    def share_copy(off):
        return pltpu.make_async_remote_copy(
            src_ref=share,
            dst_ref=shares.at[off - 1],
            send_sem=share_send.at[off - 1],
            recv_sem=share_recv.at[off - 1],
            device_id={"space": lax.rem(me_s + off, n_space)},
            device_id_type=MESH,
        )

    for off in range(1, n_space):
        share_copy(off).start()
    for off in range(1, n_space):
        share_copy(off).wait_recv()
    tables = [packed] + [shares[off - 1] for off in range(1, n_space)]
    lists = [[each[0:1, at:at + 1] for at in range(5)] for each in tables]
    norm_now = sum(each[0] for each in lists)
    centre = sum(each[0] * each[1] for each in lists) / norm_now
    spare = 0.0
    bend = 0.0
    for part_norm, part_ratio, part_spare, part_bend, part_cross in lists:
        shift = part_ratio - centre
        spare = spare + part_spare + shift * shift * part_norm
        bend = bend + part_bend + shift * (part_cross + part_spare) + shift * shift * part_ratio * part_norm
    inverse = 1.0 / centre
    norm_next = spare * inverse * inverse
    renew = norm_next / norm_now
    curve = bend * inverse * inverse - renew * norm_next * centre
    step = norm_next / curve
    of_load = inverse + step * (1.0 + renew)
    of_image = -step * inverse

    def slopes(strip, carry):
        begin = strip_of(strip)
        sides = around(strip)
        squares = [side * side for side in sides]
        load3 = three(loads, strip)
        here_stiff = stiff[pl.ds(begin + PAD, 8), :]
        held = jnp.zeros((8, columns), f32)
        bent = jnp.zeros((8, columns), f32)
        for array, push, of_rows, of_columns in (
            (image0, force0, 1.0, shear), (image1, force1, shear, 1.0)
        ):
            image3 = three(array, strip)
            above, here, below = [
                (of_load * push) * load3[at] + of_image * image3[at] for at in range(3)
            ]
            up = here - above
            down = here - below
            left = here - pltpu.roll(here, 1, 1)
            right = here - pltpu.roll(here, columns - 1, 1)
            held = held + here * here
            bent = (
                bent
                + of_rows * (squares[0] * (up * up) + squares[1] * (down * down))
                + of_columns * (squares[2] * (left * left) + squares[3] * (right * right))
            )
        bent = bent * 0.5 / jnp.maximum(here_stiff * here_stiff, 1e-6)
        gain[pl.ds(begin, 8), :] = factor[pl.ds(begin, 8), :] * (kappa_ground * held + bent)
        return carry

    lax.fori_loop(0, strips, slopes, 0)

    for at in range(kernels):
        scale = gain[...]
        sent = jnp.concatenate(
            [fields[at, pl.ds(0, span), :] * scale, -(fields[at, pl.ds(span, span), :] * scale)], axis=0
        )
        hi, lo = halves(sent)
        both = back_row_both[at][:, :2 * span]
        of_high = dot(both, hi)
        turned = of_high[:2 * rows] + of_high[2 * rows:] + dot(both[:2 * rows], lo)
        for part in range(2):
            piece = turned[part * rows:(part + 1) * rows]
            parts = [piece[:, block * LANES:(block + 1) * LANES] for block in range(blocks)]
            for block in range(blocks):
                hi, lo = halves(jnp.concatenate([parts[block], side_lanes(parts, block)], axis=1))
                lanes = pl.ds((2 * at + part) * 2 * LANES, 2 * LANES)
                back_hi[block, :, lanes] = hi
                back_lo[block, :, lanes] = lo

    width = columns // n_corner
    per_block = LANES // width
    my_block = me_c // per_block

    def term_copy(block, other, sent_as):
        slot = lax.rem(other - me_c + n_corner, n_corner) - 1
        return pltpu.make_async_remote_copy(
            src_ref=term.at[block],
            dst_ref=landed.at[slot],
            send_sem=term_send.at[sent_as],
            recv_sem=term_recv.at[slot],
            device_id={"corner": other},
            device_id_type=MESH,
        )

    sends = []
    half = blocks // 2
    ahead = [half, half - 1, half + 1, half + 2] + [at for at in range(half - 2, 0, -1)]
    ahead += [at for at in range(half + 3, blocks)] + [0]
    for group in (ahead[:half], ahead[half:]):
        places = [lax.rem(my_block + at, blocks) for at in group]
        hi = jnp.concatenate([back_hi[place] for place in places], axis=0)
        lo = jnp.concatenate([back_lo[place] for place in places], axis=0)
        wide = dot(hi, back_col[...])
        value = wide[:, :LANES] + wide[:, LANES:] + dot(lo, back_col[:, pl.ds(0, LANES)])
        for at, place in enumerate(places):
            term[place] = value[at * rows:(at + 1) * rows]
        for at, place in zip(group, places):
            for step in range(per_block):
                if at == 0 and step == 0:
                    continue
                other = place * per_block + lax.rem(me_c + step, per_block)
                copy = term_copy(place, other, len(sends))
                copy.start()
                sends.append(copy)
    summed = term[my_block]
    for off in range(1, n_corner):
        term_copy(my_block, lax.rem(me_c + off, n_corner), off - 1).wait_recv()
        summed = summed + landed[off - 1]
    if per_block == 1:
        out_ref[...] = summed
    else:
        place = lax.rem(me_c, per_block)
        kept = jnp.zeros(out_ref.shape, f32)
        for at in range(per_block):
            kept = kept + jnp.where(place == at, 1.0, 0.0) * summed[:, at * width:(at + 1) * width]
        out_ref[...] = kept

    for copy in sends:
        copy.wait_send()
    for off in range(1, n_space):
        share_copy(off).wait_send()

    @pl.when(has_before)
    def _():
        for copy in edge_copies(0):
            copy.wait_send()

    @pl.when(has_after)
    def _():
        for copy in edge_copies(1):
            copy.wait_send()


def on_device(
    n_space, n_corner,
    design, corner_set, corner_dose, kernel_taps, kernel_weights, support_mask, load_mask, force,
):
    rows, columns = design.shape
    kernels = kernel_taps.shape[2]
    radius = kernel_taps.shape[3] // 2
    span = rows + 2 * EDGE
    reach = rows + 2 * HALO
    blocks = columns // LANES
    padded_rows = span + 2 * PAD
    in_hbm = pl.BlockSpec(memory_space=pltpu.HBM)
    in_vmem = pl.BlockSpec(memory_space=pltpu.VMEM)
    scratch = [
        pltpu.SMEM(corner_set.shape, jnp.int32),
        pltpu.SMEM(corner_dose.shape, f32),
        pltpu.SMEM(kernel_weights.shape, f32),
        pltpu.SMEM(force.shape, f32),
        pltpu.VMEM(design.shape, f32),
        pltpu.VMEM(kernel_taps.shape, f32),
        pltpu.VMEM(design.shape, jnp.int32),
        pltpu.VMEM(design.shape, jnp.int32),
        pltpu.VMEM((4 * kernels, LANES), f32),
        pltpu.VMEM((4 * kernels, LANES), f32),
        pltpu.VMEM((4 * kernels, LANES), f32),
        pltpu.VMEM((kernels, 6 * LANES, 2 * LANES), bf16),
        pltpu.VMEM((kernels * 4 * LANES, 2 * LANES), bf16),
        pltpu.VMEM((kernels, 4 * span, 2 * LANES), bf16),
        pltpu.VMEM((kernels, 4 * rows, 2 * LANES), bf16),
        pltpu.VMEM((2 * HALO, columns), f32),
        pltpu.VMEM((2, 2 * MASK_HALO, columns), jnp.int32),
        pltpu.VMEM((blocks * rows, 6 * LANES), bf16),
        pltpu.VMEM((kernels, 2 * reach, columns), bf16),
        pltpu.VMEM((kernels, 2 * reach, columns), bf16),
        pltpu.VMEM((kernels, 2 * span, columns), f32),
        pltpu.VMEM((blocks, rows, kernels * 4 * LANES), bf16),
        pltpu.VMEM((blocks, rows, kernels * 4 * LANES), bf16),
        pltpu.VMEM((padded_rows, columns), f32),
        pltpu.VMEM((span, columns), f32),
        pltpu.VMEM((padded_rows, columns), f32),
        pltpu.VMEM((span, columns), f32),
        pltpu.VMEM((padded_rows, columns), f32),
        pltpu.VMEM((padded_rows, columns), f32),
        pltpu.VMEM((padded_rows, columns), f32),
        pltpu.VMEM((span, columns), f32),
        pltpu.VMEM((span, columns), f32),
        pltpu.VMEM((blocks, rows, LANES), f32),
        pltpu.VMEM((8, LANES), f32),
        pltpu.VMEM((n_space - 1, 8, LANES), f32),
        pltpu.VMEM((n_corner - 1, rows, LANES), f32),
        pltpu.SemaphoreType.DMA((8,)),
        pltpu.SemaphoreType.DMA((2, 3)),
        pltpu.SemaphoreType.DMA((2, 3)),
        pltpu.SemaphoreType.DMA((n_space - 1,)),
        pltpu.SemaphoreType.DMA((n_space - 1,)),
        pltpu.SemaphoreType.DMA((n_corner - 1,)),
        pltpu.SemaphoreType.DMA((n_corner - 1,)),
    ]
    return pl.pallas_call(
        functools.partial(kernel, n_space, n_corner, kernels, radius),
        out_shape=jax.ShapeDtypeStruct((rows, columns // n_corner), f32),
        in_specs=[in_hbm] * 8,
        out_specs=in_vmem,
        scratch_shapes=scratch,
        compiler_params=pltpu.CompilerParams(
            collective_id=0, has_side_effects=True, vmem_limit_bytes=56 * 1024 * 1024
        ),
    )(
        corner_set, corner_dose, kernel_weights, force,
        design, kernel_taps, support_mask, load_mask,
    )


def solution(mesh):
    placed = (
        P("space", None),
        P("corner"),
        P("corner"),
        P(),
        P(),
        P("space", None),
        P("space", None),
        P(),
    )
    body = functools.partial(on_device, mesh.shape["space"], mesh.shape["corner"])
    return jax.shard_map(
        body, mesh=mesh, in_specs=placed, out_specs=P("space", "corner"), check_vma=False
    )
```

```python
import functools
import math

import jax
import jax.numpy as jnp
from jax import lax
from jax.experimental import pallas as pl
from jax.experimental.pallas import tpu as pltpu
from jax.sharding import PartitionSpec as P

MESH = pl.DeviceIdType.MESH
LANES = 128
HALO = 24
TAIL = 18
MASK_HALO = 16
EDGE = 12
PAD = 8

beta_sharp = 8.0
eta_level = 0.25
stiff_floor = 0.05
kappa_ground = 0.1
shear = 0.35
bf16 = jnp.bfloat16
f32 = jnp.float32


def halves(value):
    high = value.astype(bf16)
    return high, (value - high.astype(f32)).astype(bf16)


def dot(left, right):
    return jnp.dot(left, right, preferred_element_type=f32)


def circulant(row, count, shift):
    turned = pltpu.roll(jnp.broadcast_to(row, (8, LANES)), shift, 1) if shift else row
    return pltpu.roll(
        jnp.broadcast_to(turned[:1], (count, LANES)), 0, 1, stride=1, stride_axis=0
    )


def side_lanes(blocks, at):
    zero = jnp.zeros_like(blocks[0])
    before = blocks[at - 1] if at > 0 else zero
    after = blocks[at + 1] if at + 1 < len(blocks) else zero
    lane = lax.broadcasted_iota(jnp.int32, zero.shape, 1)
    return jnp.where(lane < LANES // 2, after, before)


def kernel(
    n_space, n_corner, kernels, radius,
    set_any, dose_any, weight_any, force_any, design_any, taps_any, support_any, load_any,
    out_ref,
    set_ref, dose_ref, weight_ref, force_ref, design_ref, taps_ref, support_ref, load_ref,
    tap_rows, base_plain, base_flip,
    col_all, back_col, row_all, back_row_both,
    halo, mask_halo, wide_design, stacked, stacked16, left_all, mid, fields, back_hi, back_lo, bright,
    stiff, ground, face_dn, face_rt, loads, image0, image1, factor, gain,
    term, share, shares, landed,
    local_sem, halo_send, halo_recv, share_send, share_recv, term_send, term_recv,
):
    local = [
        pltpu.make_async_copy(source, target, local_sem.at[at])
        for at, (source, target) in enumerate((
            (taps_any, taps_ref), (set_any, set_ref), (dose_any, dose_ref), (weight_any, weight_ref),
            (force_any, force_ref), (design_any, design_ref), (load_any, load_ref), (support_any, support_ref),
        ))
    ]
    for copy in local:
        copy.start()
    rows, columns = design_ref.shape
    span = rows + 2 * EDGE
    blocks = columns // LANES
    strips = span // 8
    me_s = lax.axis_index("space")
    me_c = lax.axis_index("corner")

    barrier = pltpu.get_barrier_semaphore()
    for off in range(1, n_space):
        pl.semaphore_signal(
            barrier, inc=1, device_id={"space": lax.rem(me_s + off, n_space)}, device_id_type=MESH
        )
    for off in range(1, n_corner):
        pl.semaphore_signal(
            barrier, inc=1, device_id={"corner": lax.rem(me_c + off, n_corner)}, device_id_type=MESH
        )

    pl.semaphore_wait(barrier, n_space + n_corner - 2)

    def edge_copies(toward):
        other = lax.rem(me_s + (n_space - 1 if toward == 0 else 1), n_space)
        sent = []
        for which_one, (source, target, width) in enumerate((
            (design_any, halo, HALO),
            (load_any, mask_halo.at[0], MASK_HALO),
            (support_any, mask_halo.at[1], MASK_HALO),
        )):
            begin = 0 if toward == 0 else rows - width
            sent.append(pltpu.make_async_remote_copy(
                src_ref=source.at[pl.ds(begin, width)],
                dst_ref=target.at[pl.ds(toward * width, width)],
                send_sem=halo_send.at[toward, which_one],
                recv_sem=halo_recv.at[toward, which_one],
                device_id={"space": other},
                device_id_type=MESH,
            ))
        return sent

    has_before = me_s > 0
    has_after = me_s < n_space - 1

    @pl.when(has_before)
    def _():
        for copy in edge_copies(0):
            copy.start()

    @pl.when(has_after)
    def _():
        for copy in edge_copies(1):
            copy.start()

    for copy in local[:5]:
        copy.wait()

    chosen = set_ref[0]
    tap_rows[...] = jnp.zeros_like(tap_rows)
    for part in range(4):
        tap_rows[pl.ds(part * kernels, kernels), pl.ds(0, 2 * radius + 1)] = taps_ref[chosen, part]
    table = tap_rows[...]
    base_plain[...] = pltpu.roll(table, LANES - radius, 1)
    from_lane = lax.broadcasted_iota(jnp.int32, (LANES, LANES), 0)
    to_lane = lax.broadcasted_iota(jnp.int32, (LANES, LANES), 1)
    mirror = ((from_lane + to_lane) % LANES == radius).astype(f32)
    base_flip[...] = jnp.dot(
        table, mirror, preferred_element_type=f32, precision=lax.Precision.HIGHEST
    )
    sums = jnp.sum(table, axis=1, keepdims=True)
    sums = [sums[part * kernels:(part + 1) * kernels] for part in range(4)]
    which = lax.broadcasted_iota(jnp.int32, (kernels, 1), 0)
    weight_col = jnp.zeros((kernels, 1), f32)
    for at in range(kernels):
        weight_col = jnp.where(which == at, weight_ref[chosen, at], weight_col)
    clear = jnp.sum(
        weight_col
        * (sums[0] * sums[0] + sums[1] * sums[1])
        * (sums[2] * sums[2] + sums[3] * sums[3]),
        axis=0, keepdims=True,
    )
    dose = dose_ref[0]

    near = jnp.abs(from_lane - to_lane) <= radius
    lane_row = lax.broadcasted_iota(jnp.int32, (span, LANES), 1)
    lane_out = lax.broadcasted_iota(jnp.int32, (rows, LANES), 1)
    reach = rows + 2 * TAIL

    def build(at, carry):
        def plain(part):
            return base_plain[pl.ds(part * kernels + at, 1), :]

        def flip(part):
            return base_flip[pl.ds(part * kernels + at, 1), :]

        for part in range(2):
            band = circulant(plain(2 + part), LANES, 0)
            hi, lo = halves(band)
            zero = jnp.zeros_like(hi)
            there = pl.ds(part * LANES, LANES)
            for place, value in ((0, hi), (1, lo), (2, hi)):
                col_all[at, pl.ds(2 * place * LANES, LANES), there] = jnp.where(near, value, zero)
                col_all[at, pl.ds((2 * place + 1) * LANES, LANES), there] = jnp.where(near, zero, value)
            band = circulant(flip(2 + part), LANES, 0)
            hi, lo = halves(band)
            for value, lanes in ((hi, 0), (lo, LANES)):
                place = pl.multiple_of(at * (4 * LANES), LANES) + 2 * part * LANES
                back_col[pl.ds(place, LANES), pl.ds(lanes, LANES)] = jnp.where(near, value, zero)
                back_col[pl.ds(place + LANES, LANES), pl.ds(lanes, LANES)] = jnp.where(near, zero, value)

        def joined(first, second, lane, width):
            turned = pltpu.roll(second, width, 1)
            left = jnp.where(lane < width, first, turned)
            right = jnp.where(lane < 2 * width - LANES, turned, 0.0)
            return jnp.concatenate([left, right], axis=1)

        def forward_rows(part):
            band = circulant(flip(part), span, LANES - EDGE)
            band = jnp.where(lane_row < rows + TAIL, band, pltpu.roll(band, reach, 1))
            band = jnp.where(lane_row < reach, band, 0.0)
            hi = band.astype(bf16).astype(f32)
            second = pltpu.roll(hi, reach, 1)
            third = pltpu.roll(band - hi, 2 * reach - LANES, 1)
            left = jnp.where(lane_row < reach, hi, second)
            right = jnp.where(
                lane_row < 2 * reach - LANES, second, jnp.where(lane_row < 3 * reach - LANES, third, 0.0)
            )
            return jnp.concatenate([left, right], axis=1)

        row_all[pl.ds(pl.multiple_of(at * (2 * span), 16), 2 * span), :] = jnp.concatenate(
            [forward_rows(0), forward_rows(1)], axis=0
        ).astype(bf16)
        scale = 2.0 * weight_ref[chosen, at]
        row_re = circulant(plain(0), rows, EDGE) * scale
        row_im = circulant(plain(1), rows, EDGE) * scale
        matrix = jnp.concatenate(
            [joined(row_re, -row_im, lane_out, span), joined(-row_im, -row_re, lane_out, span)], axis=0
        )
        hi, lo = halves(matrix)
        back_row_both[at, pl.ds(0, 2 * rows), :] = hi
        back_row_both[at, pl.ds(2 * rows, 2 * rows), :] = lo
        return carry

    lax.fori_loop(0, kernels, build, 0)

    local[5].wait()
    wide_design[pl.ds(0, rows), :] = design_ref[...]

    @pl.when(has_after)
    def _():
        for copy in edge_copies(0):
            copy.wait_recv()

    @pl.when(jnp.logical_not(has_after))
    def _():
        halo[pl.ds(0, HALO), :] = jnp.zeros((HALO, columns), f32)
        mask_halo[:, pl.ds(0, MASK_HALO), :] = jnp.zeros((2, MASK_HALO, columns), jnp.int32)

    @pl.when(has_before)
    def _():
        for copy in edge_copies(1):
            copy.wait_recv()

    @pl.when(jnp.logical_not(has_before))
    def _():
        halo[pl.ds(HALO, HALO), :] = jnp.zeros((HALO, columns), f32)
        mask_halo[:, pl.ds(MASK_HALO, MASK_HALO), :] = jnp.zeros((2, MASK_HALO, columns), jnp.int32)

    wide_design[pl.ds(rows, TAIL), :] = halo[pl.ds(0, TAIL), :]
    wide_design[pl.ds(rows + TAIL, TAIL), :] = halo[pl.ds(2 * HALO - TAIL, TAIL), :]
    cells = wide_design[pl.ds(0, reach), :]
    high = cells.astype(bf16).astype(f32)
    stacked[pl.ds(0, reach), :] = high
    stacked[pl.ds(reach, reach), :] = cells - high
    stacked[pl.ds(2 * reach, reach), :] = high
    stacked[pl.ds(3 * reach, 2 * LANES - 3 * reach), :] = jnp.zeros((2 * LANES - 3 * reach, columns), f32)
    stacked16[...] = stacked[...].astype(bf16)
    for part in range(0, columns, 2 * LANES):
        lanes = pl.ds(part, 2 * LANES)
        mid[:, lanes] = dot(row_all[...], stacked16[:, lanes])

    for at in range(kernels):
        left = left_all.at[at % 2]
        value = mid[pl.ds(at * 2 * span, 2 * span), :]
        parts = [value[:, block * LANES:(block + 1) * LANES] for block in range(blocks)]
        for block in range(blocks):
            hi, lo = halves(jnp.concatenate([parts[block], side_lanes(parts, block)], axis=1))
            left[pl.ds(block * 2 * span, 2 * span), :] = jnp.concatenate([hi, hi, lo], axis=1)
        value = dot(left[...], col_all[at])
        weight = weight_ref[chosen, at]
        for block in range(blocks):
            of_re = value[block * 2 * span:block * 2 * span + span]
            of_im = value[block * 2 * span + span:(block + 1) * 2 * span]
            re = of_re[:, :LANES] - of_im[:, LANES:]
            im = of_re[:, LANES:] + of_im[:, :LANES]
            lanes = pl.ds(block * LANES, LANES)
            fields[at, pl.ds(0, span), lanes] = re
            fields[at, pl.ds(span, span), lanes] = im
            light = weight * (re * re + im * im)
            bright[:, lanes] = light if at == 0 else bright[:, lanes] + light

    for copy in local[6:]:
        copy.wait()

    zero_pad = jnp.zeros((PAD, columns), f32)
    for array in (stiff, face_dn, loads, image0, image1):
        array[pl.ds(0, PAD), :] = zero_pad
        array[pl.ds(PAD + span, PAD), :] = zero_pad
    for which_one, own, target, base in ((0, load_ref, loads, PAD), (1, support_ref, ground, 0)):
        target[pl.ds(base, EDGE), :] = mask_halo[which_one, pl.ds(2 * MASK_HALO - EDGE, EDGE), :].astype(f32)
        target[pl.ds(base + EDGE, rows), :] = own[...].astype(f32)
        target[pl.ds(base + EDGE + rows, EDGE), :] = mask_halo[which_one, pl.ds(0, EDGE), :].astype(f32)

    row_in = lax.broadcasted_iota(jnp.int32, (8, columns), 0)
    lane_in = lax.broadcasted_iota(jnp.int32, (8, columns), 1)
    first_row = me_s * rows - EDGE
    grid_rows = n_space * rows
    low_end = math.tanh(beta_sharp * eta_level)
    spread = low_end + math.tanh(beta_sharp * (1.0 - eta_level))
    level = dose / clear
    gain_scale = level * (3.0 * (1.0 - stiff_floor) * beta_sharp / spread)

    def strip_of(strip):
        return pl.multiple_of(strip * 8, 8)

    def row_above(array, begin, here):
        before = array[pl.ds(begin + PAD - 8, 8), :]
        return jnp.where(row_in == 0, pltpu.roll(before, 1, 0), pltpu.roll(here, 1, 0))

    def row_below(array, begin, here):
        after = array[pl.ds(begin + PAD + 8, 8), :]
        return jnp.where(row_in == 7, pltpu.roll(after, 7, 0), pltpu.roll(here, 7, 0))

    def project(strip, carry):
        begin = strip_of(strip)
        light = bright[pl.ds(begin, 8), :] * level
        bent = jnp.tanh(beta_sharp * (light - eta_level))
        density = (low_end + bent) * (1.0 / spread)
        square = density * density
        grid_row = row_in + (first_row + begin)
        inside = (grid_row >= 0) & (grid_row < grid_rows)
        hard = jnp.where(inside, stiff_floor + (1.0 - stiff_floor) * square * density, 0.0)
        stiff[pl.ds(begin + PAD, 8), :] = hard
        ground[pl.ds(begin, 8), :] = kappa_ground * hard + ground[pl.ds(begin, 8), :]
        factor[pl.ds(begin, 8), :] = jnp.where(
            inside, -gain_scale * square * (1.0 - bent * bent), 0.0
        )
        return carry

    lax.fori_loop(0, strips, project, 0)

    def faces(strip, carry):
        begin = strip_of(strip)
        here = stiff[pl.ds(begin + PAD, 8), :]
        below = row_below(stiff, begin, here)
        face_dn[pl.ds(begin + PAD, 8), :] = 2.0 * here * below / jnp.maximum(here + below, 1e-20)
        right = pltpu.roll(here, columns - 1, 1)
        face = 2.0 * here * right / jnp.maximum(here + right, 1e-20)
        face_rt[pl.ds(begin, 8), :] = jnp.where(lane_in < columns - 1, face, 0.0)
        return carry

    lax.fori_loop(0, strips, faces, 0)

    force0 = force_ref[0]
    force1 = force_ref[1]

    def around(strip):
        begin = strip_of(strip)
        right = face_rt[pl.ds(begin, 8), :]
        down = face_dn[pl.ds(begin + PAD, 8), :]
        return row_above(face_dn, begin, down), down, pltpu.roll(right, 1, 1), right

    def three(array, strip):
        begin = strip_of(strip)
        here = array[pl.ds(begin + PAD, 8), :]
        return row_above(array, begin, here), here, row_below(array, begin, here)

    def own_rows(strip):
        row = row_in + strip_of(strip)
        return (row >= EDGE) & (row < EDGE + rows)

    def flows(above, here, below, sides):
        face_up, face_down, face_left, face_right = sides
        along_rows = face_up * (here - above) + face_down * (here - below)
        along_columns = face_left * (here - pltpu.roll(here, 1, 1)) + face_right * (
            here - pltpu.roll(here, columns - 1, 1)
        )
        return along_rows, along_columns

    def first_image(strip, carry):
        norm, energy = carry
        begin = strip_of(strip)
        above, here, below = three(loads, strip)
        along_rows, along_columns = flows(above, here, below, around(strip))
        held = ground[pl.ds(begin, 8), :] * here
        one = force0 * (held + along_rows + shear * along_columns)
        two = force1 * (held + shear * along_rows + along_columns)
        image0[pl.ds(begin + PAD, 8), :] = one
        image1[pl.ds(begin + PAD, 8), :] = two
        own = jnp.where(own_rows(strip), here, 0.0)
        return norm + own * own, energy + own * (force0 * one + force1 * two)

    blank = jnp.zeros((8, columns), f32)
    norm, energy = lax.fori_loop(0, strips, first_image, (blank, blank))

    def whole_sum(cells):
        return jnp.sum(jnp.sum(cells, axis=0, keepdims=True), axis=1, keepdims=True)

    norm = whole_sum(norm) * (force0 * force0 + force1 * force1)
    energy = whole_sum(energy)
    ratio = jnp.where(norm > 0.0, energy / jnp.where(norm > 0.0, norm, 1.0), 0.0)

    def second_image(strip, carry):
        sums = list(carry)
        sides = around(strip)
        load3 = three(loads, strip)
        held = ground[pl.ds(strip_of(strip), 8), :]
        keep = own_rows(strip)
        for array, push, of_rows, of_columns in (
            (image0, force0, 1.0, shear), (image1, force1, shear, 1.0)
        ):
            image3 = three(array, strip)
            lean = ratio * push
            above, here, below = [image3[at] - lean * load3[at] for at in range(3)]
            along_rows, along_columns = flows(above, here, below, sides)
            applied = held * here + of_rows * along_rows + of_columns * along_columns
            applied = jnp.where(keep, applied, 0.0)
            sums[0] = sums[0] + jnp.where(keep, here * here, 0.0)
            sums[1] = sums[1] + here * applied
            sums[2] = sums[2] + push * load3[1] * applied
        return tuple(sums)

    first_strip = EDGE // 8
    last_strip = (EDGE + rows + 7) // 8
    rest = lax.fori_loop(first_strip, last_strip, second_image, (blank, blank, blank))
    values = [norm, ratio] + [whole_sum(cells) for cells in rest]
    lane8 = lax.broadcasted_iota(jnp.int32, (8, LANES), 1)
    packed = jnp.zeros((8, LANES), f32)
    for at, value in enumerate(values):
        packed = jnp.where(lane8 == at, value, packed)
    share[...] = packed

    def share_copy(off):
        return pltpu.make_async_remote_copy(
            src_ref=share,
            dst_ref=shares.at[off - 1],
            send_sem=share_send.at[off - 1],
            recv_sem=share_recv.at[off - 1],
            device_id={"space": lax.rem(me_s + off, n_space)},
            device_id_type=MESH,
        )

    for off in range(1, n_space):
        share_copy(off).start()
    for off in range(1, n_space):
        share_copy(off).wait_recv()
    tables = [packed] + [shares[off - 1] for off in range(1, n_space)]
    lists = [[each[0:1, at:at + 1] for at in range(5)] for each in tables]
    norm_now = sum(each[0] for each in lists)
    centre = sum(each[0] * each[1] for each in lists) / norm_now
    spare = 0.0
    bend = 0.0
    for part_norm, part_ratio, part_spare, part_bend, part_cross in lists:
        shift = part_ratio - centre
        spare = spare + part_spare + shift * shift * part_norm
        bend = bend + part_bend + shift * (part_cross + part_spare) + shift * shift * part_ratio * part_norm
    inverse = 1.0 / centre
    norm_next = spare * inverse * inverse
    renew = norm_next / norm_now
    curve = bend * inverse * inverse - renew * norm_next * centre
    step = norm_next / curve
    of_load = inverse + step * (1.0 + renew)
    of_image = -step * inverse

    def slopes(strip, carry):
        begin = strip_of(strip)
        sides = around(strip)
        squares = [side * side for side in sides]
        load3 = three(loads, strip)
        here_stiff = stiff[pl.ds(begin + PAD, 8), :]
        held = jnp.zeros((8, columns), f32)
        bent = jnp.zeros((8, columns), f32)
        for array, push, of_rows, of_columns in (
            (image0, force0, 1.0, shear), (image1, force1, shear, 1.0)
        ):
            image3 = three(array, strip)
            above, here, below = [
                (of_load * push) * load3[at] + of_image * image3[at] for at in range(3)
            ]
            up = here - above
            down = here - below
            left = here - pltpu.roll(here, 1, 1)
            right = here - pltpu.roll(here, columns - 1, 1)
            held = held + here * here
            bent = (
                bent
                + of_rows * (squares[0] * (up * up) + squares[1] * (down * down))
                + of_columns * (squares[2] * (left * left) + squares[3] * (right * right))
            )
        bent = bent * 0.5 / jnp.maximum(here_stiff * here_stiff, 1e-6)
        gain[pl.ds(begin, 8), :] = factor[pl.ds(begin, 8), :] * (kappa_ground * held + bent)
        return carry

    lax.fori_loop(0, strips, slopes, 0)

    for at in range(kernels):
        scale = gain[...]
        sent = jnp.concatenate(
            [fields[at, pl.ds(0, span), :] * scale, -(fields[at, pl.ds(span, span), :] * scale)], axis=0
        )
        hi, lo = halves(sent)
        both = back_row_both[at][:, :2 * span]
        of_high = dot(both, hi)
        turned = of_high[:2 * rows] + of_high[2 * rows:] + dot(both[:2 * rows], lo)
        for part in range(2):
            piece = turned[part * rows:(part + 1) * rows]
            parts = [piece[:, block * LANES:(block + 1) * LANES] for block in range(blocks)]
            for block in range(blocks):
                hi, lo = halves(jnp.concatenate([parts[block], side_lanes(parts, block)], axis=1))
                lanes = pl.ds((2 * at + part) * 2 * LANES, 2 * LANES)
                back_hi[block, :, lanes] = hi
                back_lo[block, :, lanes] = lo

    width = columns // n_corner
    per_block = LANES // width
    my_block = me_c // per_block

    def term_copy(block, other, sent_as):
        slot = lax.rem(other - me_c + n_corner, n_corner) - 1
        return pltpu.make_async_remote_copy(
            src_ref=term.at[block],
            dst_ref=landed.at[slot],
            send_sem=term_send.at[sent_as],
            recv_sem=term_recv.at[slot],
            device_id={"corner": other},
            device_id_type=MESH,
        )

    sends = []
    half = blocks // 2
    ahead = [half, half - 1, half + 1, half + 2] + [at for at in range(half - 2, 0, -1)]
    ahead += [at for at in range(half + 3, blocks)] + [0]
    for group in (ahead[:half], ahead[half:]):
        places = [lax.rem(my_block + at, blocks) for at in group]
        hi = jnp.concatenate([back_hi[place] for place in places], axis=0)
        lo = jnp.concatenate([back_lo[place] for place in places], axis=0)
        wide = dot(hi, back_col[...])
        value = wide[:, :LANES] + wide[:, LANES:] + dot(lo, back_col[:, pl.ds(0, LANES)])
        for at, place in enumerate(places):
            term[place] = value[at * rows:(at + 1) * rows]
        for at, place in zip(group, places):
            for step in range(per_block):
                if at == 0 and step == 0:
                    continue
                other = place * per_block + lax.rem(me_c + step, per_block)
                copy = term_copy(place, other, len(sends))
                copy.start()
                sends.append(copy)
    summed = term[my_block]
    for off in range(1, n_corner):
        term_copy(my_block, lax.rem(me_c + off, n_corner), off - 1).wait_recv()
        summed = summed + landed[off - 1]
    if per_block == 1:
        out_ref[...] = summed
    else:
        place = lax.rem(me_c, per_block)
        kept = jnp.zeros(out_ref.shape, f32)
        for at in range(per_block):
            kept = kept + jnp.where(place == at, 1.0, 0.0) * summed[:, at * width:(at + 1) * width]
        out_ref[...] = kept

    for copy in sends:
        copy.wait_send()
    for off in range(1, n_space):
        share_copy(off).wait_send()

    @pl.when(has_before)
    def _():
        for copy in edge_copies(0):
            copy.wait_send()

    @pl.when(has_after)
    def _():
        for copy in edge_copies(1):
            copy.wait_send()


def on_device(
    n_space, n_corner,
    design, corner_set, corner_dose, kernel_taps, kernel_weights, support_mask, load_mask, force,
):
    rows, columns = design.shape
    kernels = kernel_taps.shape[2]
    radius = kernel_taps.shape[3] // 2
    span = rows + 2 * EDGE
    blocks = columns // LANES
    padded_rows = span + 2 * PAD
    in_hbm = pl.BlockSpec(memory_space=pltpu.HBM)
    in_vmem = pl.BlockSpec(memory_space=pltpu.VMEM)
    scratch = [
        pltpu.SMEM(corner_set.shape, jnp.int32),
        pltpu.SMEM(corner_dose.shape, f32),
        pltpu.SMEM(kernel_weights.shape, f32),
        pltpu.SMEM(force.shape, f32),
        pltpu.VMEM(design.shape, f32),
        pltpu.VMEM(kernel_taps.shape, f32),
        pltpu.VMEM(design.shape, jnp.int32),
        pltpu.VMEM(design.shape, jnp.int32),
        pltpu.VMEM((4 * kernels, LANES), f32),
        pltpu.VMEM((4 * kernels, LANES), f32),
        pltpu.VMEM((4 * kernels, LANES), f32),
        pltpu.VMEM((kernels, 6 * LANES, 2 * LANES), bf16),
        pltpu.VMEM((kernels * 4 * LANES, 2 * LANES), bf16),
        pltpu.VMEM((kernels * 2 * span, 2 * LANES), bf16),
        pltpu.VMEM((kernels, 4 * rows, 2 * LANES), bf16),
        pltpu.VMEM((2 * HALO, columns), f32),
        pltpu.VMEM((2, 2 * MASK_HALO, columns), jnp.int32),
        pltpu.VMEM((rows + 2 * HALO, columns), f32),
        pltpu.VMEM((2 * LANES, columns), f32),
        pltpu.VMEM((2 * LANES, columns), bf16),
        pltpu.VMEM((2, blocks * 2 * span, 6 * LANES), bf16),
        pltpu.VMEM((kernels * 2 * span, columns), f32),
        pltpu.VMEM((kernels, 2 * span, columns), f32),
        pltpu.VMEM((blocks, rows, kernels * 4 * LANES), bf16),
        pltpu.VMEM((blocks, rows, kernels * 4 * LANES), bf16),
        pltpu.VMEM((span, columns), f32),
        pltpu.VMEM((padded_rows, columns), f32),
        pltpu.VMEM((span, columns), f32),
        pltpu.VMEM((padded_rows, columns), f32),
        pltpu.VMEM((span, columns), f32),
        pltpu.VMEM((padded_rows, columns), f32),
        pltpu.VMEM((padded_rows, columns), f32),
        pltpu.VMEM((padded_rows, columns), f32),
        pltpu.VMEM((span, columns), f32),
        pltpu.VMEM((span, columns), f32),
        pltpu.VMEM((blocks, rows, LANES), f32),
        pltpu.VMEM((8, LANES), f32),
        pltpu.VMEM((n_space - 1, 8, LANES), f32),
        pltpu.VMEM((n_corner - 1, rows, LANES), f32),
        pltpu.SemaphoreType.DMA((8,)),
        pltpu.SemaphoreType.DMA((2, 3)),
        pltpu.SemaphoreType.DMA((2, 3)),
        pltpu.SemaphoreType.DMA((n_space - 1,)),
        pltpu.SemaphoreType.DMA((n_space - 1,)),
        pltpu.SemaphoreType.DMA((n_corner - 1,)),
        pltpu.SemaphoreType.DMA((n_corner - 1,)),
    ]
    return pl.pallas_call(
        functools.partial(kernel, n_space, n_corner, kernels, radius),
        out_shape=jax.ShapeDtypeStruct((rows, columns // n_corner), f32),
        in_specs=[in_hbm] * 8,
        out_specs=in_vmem,
        scratch_shapes=scratch,
        compiler_params=pltpu.CompilerParams(
            collective_id=0, has_side_effects=True, vmem_limit_bytes=56 * 1024 * 1024
        ),
    )(
        corner_set, corner_dose, kernel_weights, force,
        design, kernel_taps, support_mask, load_mask,
    )


def solution(mesh):
    placed = (
        P("space", None),
        P("corner"),
        P("corner"),
        P(),
        P(),
        P("space", None),
        P("space", None),
        P(),
    )
    body = functools.partial(on_device, mesh.shape["space"], mesh.shape["corner"])
    return jax.shard_map(
        body, mesh=mesh, in_specs=placed, out_specs=P("space", "corner"), check_vma=False
    )
```

```python
import functools
import math

import jax
import jax.numpy as jnp
from jax import lax
from jax.experimental import pallas as pl
from jax.experimental.pallas import tpu as pltpu
from jax.sharding import PartitionSpec as P

MESH = pl.DeviceIdType.MESH
LANES = 128
HALO = 24
MASK_HALO = 16
EDGE = 12
PAD = 8

beta_sharp = 8.0
eta_level = 0.25
stiff_floor = 0.05
kappa_ground = 0.1
shear = 0.35
bf16 = jnp.bfloat16
f32 = jnp.float32


def halves(value):
    high = value.astype(bf16)
    return high, (value - high.astype(f32)).astype(bf16)


def dot(left, right):
    return jnp.dot(left, right, preferred_element_type=f32)


def circulant(row, count, shift):
    turned = pltpu.roll(jnp.broadcast_to(row, (8, LANES)), shift, 1) if shift else row
    return pltpu.roll(
        jnp.broadcast_to(turned[:1], (count, LANES)), 0, 1, stride=1, stride_axis=0
    )


def side_lanes(blocks, at):
    zero = jnp.zeros_like(blocks[0])
    before = blocks[at - 1] if at > 0 else zero
    after = blocks[at + 1] if at + 1 < len(blocks) else zero
    lane = lax.broadcasted_iota(jnp.int32, zero.shape, 1)
    return jnp.where(lane < LANES // 2, after, before)


def kernel(
    n_space, n_corner, kernels, radius,
    set_any, dose_any, weight_any, force_any, design_any, taps_any, support_any, load_any,
    out_ref,
    set_ref, dose_ref, weight_ref, force_ref, design_ref, taps_ref, support_ref, load_ref,
    tap_rows, base_plain, base_flip,
    col_all, back_col, row_both, back_row_both,
    halo, mask_halo, left_all, mid_hi, mid_lo, fields, back_hi, back_lo, sides_held, bright,
    stiff, ground, face_dn, face_rt, loads, image0, image1, factor, gain,
    term, share, shares, landed,
    local_sem, halo_send, halo_recv, share_send, share_recv, term_send, term_recv,
):
    local = [
        pltpu.make_async_copy(source, target, local_sem.at[at])
        for at, (source, target) in enumerate((
            (taps_any, taps_ref), (set_any, set_ref), (dose_any, dose_ref), (weight_any, weight_ref),
            (force_any, force_ref), (design_any, design_ref), (load_any, load_ref), (support_any, support_ref),
        ))
    ]
    for copy in local:
        copy.start()
    rows, columns = design_ref.shape
    span = rows + 2 * EDGE
    blocks = columns // LANES
    strips = span // 8
    me_s = lax.axis_index("space")
    me_c = lax.axis_index("corner")

    barrier = pltpu.get_barrier_semaphore()
    for off in range(1, n_space):
        pl.semaphore_signal(
            barrier, inc=1, device_id={"space": lax.rem(me_s + off, n_space)}, device_id_type=MESH
        )
    for off in range(1, n_corner):
        pl.semaphore_signal(
            barrier, inc=1, device_id={"corner": lax.rem(me_c + off, n_corner)}, device_id_type=MESH
        )

    pl.semaphore_wait(barrier, n_space + n_corner - 2)

    def edge_copies(toward):
        other = lax.rem(me_s + (n_space - 1 if toward == 0 else 1), n_space)
        sent = []
        for which_one, (source, target, width) in enumerate((
            (design_any, halo, HALO),
            (load_any, mask_halo.at[0], MASK_HALO),
            (support_any, mask_halo.at[1], MASK_HALO),
        )):
            begin = 0 if toward == 0 else rows - width
            sent.append(pltpu.make_async_remote_copy(
                src_ref=source.at[pl.ds(begin, width)],
                dst_ref=target.at[pl.ds(toward * width, width)],
                send_sem=halo_send.at[toward, which_one],
                recv_sem=halo_recv.at[toward, which_one],
                device_id={"space": other},
                device_id_type=MESH,
            ))
        return sent

    has_before = me_s > 0
    has_after = me_s < n_space - 1

    @pl.when(has_before)
    def _():
        for copy in edge_copies(0):
            copy.start()

    @pl.when(has_after)
    def _():
        for copy in edge_copies(1):
            copy.start()

    for copy in local[:5]:
        copy.wait()

    chosen = set_ref[0]
    tap_rows[...] = jnp.zeros_like(tap_rows)
    for part in range(4):
        tap_rows[pl.ds(part * kernels, kernels), pl.ds(0, 2 * radius + 1)] = taps_ref[chosen, part]
    table = tap_rows[...]
    base_plain[...] = pltpu.roll(table, LANES - radius, 1)
    from_lane = lax.broadcasted_iota(jnp.int32, (LANES, LANES), 0)
    to_lane = lax.broadcasted_iota(jnp.int32, (LANES, LANES), 1)
    mirror = ((from_lane + to_lane) % LANES == radius).astype(f32)
    base_flip[...] = jnp.dot(
        table, mirror, preferred_element_type=f32, precision=lax.Precision.HIGHEST
    )
    sums = jnp.sum(table, axis=1, keepdims=True)
    sums = [sums[part * kernels:(part + 1) * kernels] for part in range(4)]
    which = lax.broadcasted_iota(jnp.int32, (kernels, 1), 0)
    weight_col = jnp.zeros((kernels, 1), f32)
    for at in range(kernels):
        weight_col = jnp.where(which == at, weight_ref[chosen, at], weight_col)
    clear = jnp.sum(
        weight_col
        * (sums[0] * sums[0] + sums[1] * sums[1])
        * (sums[2] * sums[2] + sums[3] * sums[3]),
        axis=0, keepdims=True,
    )
    dose = dose_ref[0]

    near = jnp.abs(from_lane - to_lane) <= radius
    lane_row = lax.broadcasted_iota(jnp.int32, (span, LANES), 1)
    lane_out = lax.broadcasted_iota(jnp.int32, (rows, LANES), 1)
    reach = rows + 2 * HALO

    def build(at, carry):
        def plain(part):
            return base_plain[pl.ds(part * kernels + at, 1), :]

        def flip(part):
            return base_flip[pl.ds(part * kernels + at, 1), :]

        for part in range(2):
            there = pl.ds(part * LANES, LANES)
            band = circulant(plain(2 + part), LANES, 0)
            hi = band.astype(bf16).astype(f32)
            lo = band - hi
            far_hi = jnp.where(near, 0.0, hi)
            far_lo = jnp.where(near, 0.0, lo)
            near_hi = jnp.where(near, hi, 0.0).astype(bf16)
            col_all[at, pl.ds(0, LANES), there] = near_hi
            col_all[at, pl.ds(LANES, LANES), there] = near_hi
            col_all[at, pl.ds(2 * LANES, LANES), there] = jnp.where(near, lo, 0.0).astype(bf16)
            col_all[at, pl.ds(3 * LANES, LANES), there] = (
                far_hi + pltpu.roll(far_hi, 2 * radius, 0) + pltpu.roll(far_lo, 4 * radius, 0)
            ).astype(bf16)
            band = circulant(flip(2 + part), LANES, 0)
            hi = band.astype(bf16).astype(f32)
            lo = band - hi
            field = 2 * at + part
            begin = pl.multiple_of(field * LANES, LANES)
            back_col[pl.ds(begin, LANES), pl.ds(0, LANES)] = jnp.where(near, hi, 0.0).astype(bf16)
            back_col[pl.ds(begin, LANES), pl.ds(LANES, LANES)] = jnp.where(near, lo, 0.0).astype(bf16)
            far = jnp.concatenate([jnp.where(near, 0.0, hi), jnp.where(near, 0.0, lo)], axis=1)
            far = jnp.concatenate([far[LANES - radius:], far[:radius]], axis=0)
            begin = pl.multiple_of(2 * kernels * LANES + field * 2 * radius, 2 * radius)
            back_col[pl.ds(begin, 2 * radius), :] = far.astype(bf16)
            back_col[pl.ds(begin + 4 * kernels * radius, 2 * radius), pl.ds(0, LANES)] = (
                far[:, :LANES].astype(bf16)
            )
            back_col[pl.ds(begin + 4 * kernels * radius, 2 * radius), pl.ds(LANES, LANES)] = (
                jnp.zeros((2 * radius, LANES), bf16)
            )

        def joined(first, second, lane, width):
            turned = pltpu.roll(second, width, 1)
            left = jnp.where(lane < width, first, turned)
            right = jnp.where(lane < 2 * width - LANES, turned, 0.0)
            return jnp.concatenate([left, right], axis=1)

        def forward_rows(part):
            band = circulant(flip(part), span, LANES - EDGE)
            band = jnp.where(lane_row < rows + HALO, band, pltpu.roll(band, reach, 1))
            return jnp.where(lane_row < reach, band, 0.0)

        row_re = forward_rows(0)
        row_im = forward_rows(1)
        matrix = jnp.concatenate(
            [joined(row_re, -row_im, lane_row, reach), joined(row_im, row_re, lane_row, reach)], axis=0
        )
        hi, lo = halves(matrix)
        row_both[at, pl.ds(0, 2 * span), :] = hi
        row_both[at, pl.ds(2 * span, 2 * span), :] = lo
        scale = 2.0 * weight_ref[chosen, at]
        row_re = circulant(plain(0), rows, EDGE) * scale
        row_im = circulant(plain(1), rows, EDGE) * scale
        matrix = jnp.concatenate(
            [joined(row_re, -row_im, lane_out, span), joined(-row_im, -row_re, lane_out, span)], axis=0
        )
        hi, lo = halves(matrix)
        back_row_both[at, pl.ds(0, 2 * rows), :] = hi
        back_row_both[at, pl.ds(2 * rows, 2 * rows), :] = lo
        return carry

    lax.fori_loop(0, kernels, build, 0)

    def columns_of(cells, begin):
        parts = [cells[:, at * LANES:(at + 1) * LANES] for at in range(blocks)]
        for at in range(blocks):
            hi, lo = halves(parts[at])
            side = side_lanes(parts, at)
            side_hi = side.astype(bf16).astype(f32)
            packed = jnp.where(
                (lane_out < radius) | (lane_out >= LANES - radius),
                side_hi,
                jnp.where(
                    lane_out < 3 * radius,
                    pltpu.roll(side - side_hi, 2 * radius, 1),
                    jnp.where(lane_out < 5 * radius, pltpu.roll(side_hi, 4 * radius, 1), 0.0),
                ),
            )
            left_all[pl.ds(at * rows, rows), :] = jnp.concatenate([hi, lo, hi, packed.astype(bf16)], axis=1)

        for at in range(kernels):
            value = dot(left_all[...], col_all[at])
            hi, lo = halves(value)
            for block in range(blocks):
                for part in range(2):
                    here = (slice(block * rows, (block + 1) * rows), slice(part * LANES, (part + 1) * LANES))
                    there = (at, pl.ds(part * reach + begin, rows), pl.ds(block * LANES, LANES))
                    mid_hi[there] = hi[here]
                    mid_lo[there] = lo[here]

    local[5].wait()
    columns_of(design_ref[...], 0)

    @pl.when(has_after)
    def _():
        for copy in edge_copies(0):
            copy.wait_recv()

    @pl.when(jnp.logical_not(has_after))
    def _():
        halo[pl.ds(0, HALO), :] = jnp.zeros((HALO, columns), f32)
        mask_halo[:, pl.ds(0, MASK_HALO), :] = jnp.zeros((2, MASK_HALO, columns), jnp.int32)

    @pl.when(has_before)
    def _():
        for copy in edge_copies(1):
            copy.wait_recv()

    @pl.when(jnp.logical_not(has_before))
    def _():
        halo[pl.ds(HALO, HALO), :] = jnp.zeros((HALO, columns), f32)
        mask_halo[:, pl.ds(MASK_HALO, MASK_HALO), :] = jnp.zeros((2, MASK_HALO, columns), jnp.int32)

    columns_of(halo[...], rows)

    for at in range(kernels):
        both = row_both[at][:, :2 * reach]
        of_high = dot(both, mid_hi[at])
        value = of_high[:2 * span] + of_high[2 * span:] + dot(both[:2 * span], mid_lo[at])
        fields[at] = value
        light = weight_ref[chosen, at] * (value[:span] * value[:span] + value[span:] * value[span:])
        bright[...] = light if at == 0 else bright[...] + light

    for copy in local[6:]:
        copy.wait()

    zero_pad = jnp.zeros((PAD, columns), f32)
    for array in (stiff, face_dn, loads, image0, image1):
        array[pl.ds(0, PAD), :] = zero_pad
        array[pl.ds(PAD + span, PAD), :] = zero_pad
    for which_one, own, target, base in ((0, load_ref, loads, PAD), (1, support_ref, ground, 0)):
        target[pl.ds(base, EDGE), :] = mask_halo[which_one, pl.ds(2 * MASK_HALO - EDGE, EDGE), :].astype(f32)
        target[pl.ds(base + EDGE, rows), :] = own[...].astype(f32)
        target[pl.ds(base + EDGE + rows, EDGE), :] = mask_halo[which_one, pl.ds(0, EDGE), :].astype(f32)

    row_in = lax.broadcasted_iota(jnp.int32, (8, columns), 0)
    lane_in = lax.broadcasted_iota(jnp.int32, (8, columns), 1)
    first_row = me_s * rows - EDGE
    grid_rows = n_space * rows
    low_end = math.tanh(beta_sharp * eta_level)
    spread = low_end + math.tanh(beta_sharp * (1.0 - eta_level))
    level = dose / clear
    gain_scale = level * (3.0 * (1.0 - stiff_floor) * beta_sharp / spread)

    def strip_of(strip):
        return pl.multiple_of(strip * 8, 8)

    def row_above(array, begin, here):
        before = array[pl.ds(begin + PAD - 8, 8), :]
        return jnp.where(row_in == 0, pltpu.roll(before, 1, 0), pltpu.roll(here, 1, 0))

    def row_below(array, begin, here):
        after = array[pl.ds(begin + PAD + 8, 8), :]
        return jnp.where(row_in == 7, pltpu.roll(after, 7, 0), pltpu.roll(here, 7, 0))

    def project(strip, carry):
        begin = strip_of(strip)
        light = bright[pl.ds(begin, 8), :] * level
        bent = jnp.tanh(beta_sharp * (light - eta_level))
        density = (low_end + bent) * (1.0 / spread)
        square = density * density
        grid_row = row_in + (first_row + begin)
        inside = (grid_row >= 0) & (grid_row < grid_rows)
        hard = jnp.where(inside, stiff_floor + (1.0 - stiff_floor) * square * density, 0.0)
        stiff[pl.ds(begin + PAD, 8), :] = hard
        ground[pl.ds(begin, 8), :] = kappa_ground * hard + ground[pl.ds(begin, 8), :]
        factor[pl.ds(begin, 8), :] = jnp.where(
            inside, -gain_scale * square * (1.0 - bent * bent), 0.0
        )
        return carry

    lax.fori_loop(0, strips, project, 0)

    def faces(strip, carry):
        begin = strip_of(strip)
        here = stiff[pl.ds(begin + PAD, 8), :]
        below = row_below(stiff, begin, here)
        face_dn[pl.ds(begin + PAD, 8), :] = 2.0 * here * below / jnp.maximum(here + below, 1e-20)
        right = pltpu.roll(here, columns - 1, 1)
        face = 2.0 * here * right / jnp.maximum(here + right, 1e-20)
        face_rt[pl.ds(begin, 8), :] = jnp.where(lane_in < columns - 1, face, 0.0)
        return carry

    lax.fori_loop(0, strips, faces, 0)

    force0 = force_ref[0]
    force1 = force_ref[1]

    def around(strip):
        begin = strip_of(strip)
        right = face_rt[pl.ds(begin, 8), :]
        down = face_dn[pl.ds(begin + PAD, 8), :]
        return row_above(face_dn, begin, down), down, pltpu.roll(right, 1, 1), right

    def three(array, strip):
        begin = strip_of(strip)
        here = array[pl.ds(begin + PAD, 8), :]
        return row_above(array, begin, here), here, row_below(array, begin, here)

    def own_rows(strip):
        row = row_in + strip_of(strip)
        return (row >= EDGE) & (row < EDGE + rows)

    def flows(above, here, below, sides):
        face_up, face_down, face_left, face_right = sides
        along_rows = face_up * (here - above) + face_down * (here - below)
        along_columns = face_left * (here - pltpu.roll(here, 1, 1)) + face_right * (
            here - pltpu.roll(here, columns - 1, 1)
        )
        return along_rows, along_columns

    def first_image(strip, carry):
        norm, energy = carry
        begin = strip_of(strip)
        above, here, below = three(loads, strip)
        along_rows, along_columns = flows(above, here, below, around(strip))
        held = ground[pl.ds(begin, 8), :] * here
        one = force0 * (held + along_rows + shear * along_columns)
        two = force1 * (held + shear * along_rows + along_columns)
        image0[pl.ds(begin + PAD, 8), :] = one
        image1[pl.ds(begin + PAD, 8), :] = two
        own = jnp.where(own_rows(strip), here, 0.0)
        return norm + own * own, energy + own * (force0 * one + force1 * two)

    blank = jnp.zeros((8, columns), f32)
    norm, energy = lax.fori_loop(0, strips, first_image, (blank, blank))

    def whole_sum(cells):
        return jnp.sum(jnp.sum(cells, axis=0, keepdims=True), axis=1, keepdims=True)

    norm = whole_sum(norm) * (force0 * force0 + force1 * force1)
    energy = whole_sum(energy)
    ratio = jnp.where(norm > 0.0, energy / jnp.where(norm > 0.0, norm, 1.0), 0.0)

    def second_image(strip, carry):
        sums = list(carry)
        sides = around(strip)
        load3 = three(loads, strip)
        held = ground[pl.ds(strip_of(strip), 8), :]
        keep = own_rows(strip)
        for array, push, of_rows, of_columns in (
            (image0, force0, 1.0, shear), (image1, force1, shear, 1.0)
        ):
            image3 = three(array, strip)
            lean = ratio * push
            above, here, below = [image3[at] - lean * load3[at] for at in range(3)]
            along_rows, along_columns = flows(above, here, below, sides)
            applied = held * here + of_rows * along_rows + of_columns * along_columns
            applied = jnp.where(keep, applied, 0.0)
            sums[0] = sums[0] + jnp.where(keep, here * here, 0.0)
            sums[1] = sums[1] + here * applied
            sums[2] = sums[2] + push * load3[1] * applied
        return tuple(sums)

    first_strip = EDGE // 8
    last_strip = (EDGE + rows + 7) // 8
    rest = lax.fori_loop(first_strip, last_strip, second_image, (blank, blank, blank))
    values = [norm, ratio] + [whole_sum(cells) for cells in rest]
    lane8 = lax.broadcasted_iota(jnp.int32, (8, LANES), 1)
    packed = jnp.zeros((8, LANES), f32)
    for at, value in enumerate(values):
        packed = jnp.where(lane8 == at, value, packed)
    share[...] = packed

    def share_copy(off):
        return pltpu.make_async_remote_copy(
            src_ref=share,
            dst_ref=shares.at[off - 1],
            send_sem=share_send.at[off - 1],
            recv_sem=share_recv.at[off - 1],
            device_id={"space": lax.rem(me_s + off, n_space)},
            device_id_type=MESH,
        )

    for off in range(1, n_space):
        share_copy(off).start()
    for off in range(1, n_space):
        share_copy(off).wait_recv()
    tables = [packed] + [shares[off - 1] for off in range(1, n_space)]
    lists = [[each[0:1, at:at + 1] for at in range(5)] for each in tables]
    norm_now = sum(each[0] for each in lists)
    centre = sum(each[0] * each[1] for each in lists) / norm_now
    spare = 0.0
    bend = 0.0
    for part_norm, part_ratio, part_spare, part_bend, part_cross in lists:
        shift = part_ratio - centre
        spare = spare + part_spare + shift * shift * part_norm
        bend = bend + part_bend + shift * (part_cross + part_spare) + shift * shift * part_ratio * part_norm
    inverse = 1.0 / centre
    norm_next = spare * inverse * inverse
    renew = norm_next / norm_now
    curve = bend * inverse * inverse - renew * norm_next * centre
    step = norm_next / curve
    of_load = inverse + step * (1.0 + renew)
    of_image = -step * inverse

    def slopes(strip, carry):
        begin = strip_of(strip)
        sides = around(strip)
        squares = [side * side for side in sides]
        load3 = three(loads, strip)
        here_stiff = stiff[pl.ds(begin + PAD, 8), :]
        held = jnp.zeros((8, columns), f32)
        bent = jnp.zeros((8, columns), f32)
        for array, push, of_rows, of_columns in (
            (image0, force0, 1.0, shear), (image1, force1, shear, 1.0)
        ):
            image3 = three(array, strip)
            above, here, below = [
                (of_load * push) * load3[at] + of_image * image3[at] for at in range(3)
            ]
            up = here - above
            down = here - below
            left = here - pltpu.roll(here, 1, 1)
            right = here - pltpu.roll(here, columns - 1, 1)
            held = held + here * here
            bent = (
                bent
                + of_rows * (squares[0] * (up * up) + squares[1] * (down * down))
                + of_columns * (squares[2] * (left * left) + squares[3] * (right * right))
            )
        bent = bent * 0.5 / jnp.maximum(here_stiff * here_stiff, 1e-6)
        gain[pl.ds(begin, 8), :] = factor[pl.ds(begin, 8), :] * (kappa_ground * held + bent)
        return carry

    lax.fori_loop(0, strips, slopes, 0)

    for at in range(kernels):
        scale = gain[...]
        sent = jnp.concatenate(
            [fields[at, pl.ds(0, span), :] * scale, -(fields[at, pl.ds(span, span), :] * scale)], axis=0
        )
        hi, lo = halves(sent)
        both = back_row_both[at][:, :2 * span]
        of_high = dot(both, hi)
        turned = of_high[:2 * rows] + of_high[2 * rows:] + dot(both[:2 * rows], lo)
        for part in range(2):
            piece = turned[part * rows:(part + 1) * rows]
            parts = [piece[:, block * LANES:(block + 1) * LANES] for block in range(blocks)]
            for block in range(blocks):
                field = 2 * at + part
                hi, lo = halves(parts[block])
                lanes = pl.ds(field * LANES, LANES)
                back_hi[block, :, lanes] = hi
                back_lo[block, :, lanes] = lo
                edge = side_lanes(parts, block)
                edge_hi = edge.astype(bf16).astype(f32)
                slots = LANES // (2 * radius)
                place = field % slots
                turn = radius + place * 2 * radius
                keep = lane_out // (2 * radius) == place
                for group, cells in ((field // slots, edge_hi), (2 * kernels // slots + field // slots, edge - edge_hi)):
                    moved = pltpu.roll(cells, turn % LANES, 1)
                    lanes = pl.ds(group * LANES, LANES)
                    moved = jnp.where(keep, moved, 0.0 if place == 0 else sides_held[block, :, lanes])
                    if place == slots - 1:
                        lanes = pl.ds((2 * kernels + group) * LANES, LANES)
                        back_hi[block, :, lanes] = moved.astype(bf16)
                    else:
                        sides_held[block, :, lanes] = moved

    width = columns // n_corner
    per_block = LANES // width
    my_block = me_c // per_block

    def term_copy(block, other, sent_as):
        slot = lax.rem(other - me_c + n_corner, n_corner) - 1
        return pltpu.make_async_remote_copy(
            src_ref=term.at[block],
            dst_ref=landed.at[slot],
            send_sem=term_send.at[sent_as],
            recv_sem=term_recv.at[slot],
            device_id={"corner": other},
            device_id_type=MESH,
        )

    sends = []
    half = blocks // 2
    ahead = [half, half - 1, half + 1, half + 2] + [at for at in range(half - 2, 0, -1)]
    ahead += [at for at in range(half + 3, blocks)] + [0]
    for group in (ahead[:half], ahead[half:]):
        places = [lax.rem(my_block + at, blocks) for at in group]
        hi = jnp.concatenate([back_hi[place] for place in places], axis=0)
        lo = jnp.concatenate([back_lo[place] for place in places], axis=0)
        wide = dot(hi, back_col[...])
        value = wide[:, :LANES] + wide[:, LANES:] + dot(lo, back_col[pl.ds(0, 2 * kernels * LANES), pl.ds(0, LANES)])
        for at, place in enumerate(places):
            term[place] = value[at * rows:(at + 1) * rows]
        for at, place in zip(group, places):
            for step in range(per_block):
                if at == 0 and step == 0:
                    continue
                other = place * per_block + lax.rem(me_c + step, per_block)
                copy = term_copy(place, other, len(sends))
                copy.start()
                sends.append(copy)
    summed = term[my_block]
    for off in range(1, n_corner):
        term_copy(my_block, lax.rem(me_c + off, n_corner), off - 1).wait_recv()
        summed = summed + landed[off - 1]
    if per_block == 1:
        out_ref[...] = summed
    else:
        place = lax.rem(me_c, per_block)
        kept = jnp.zeros(out_ref.shape, f32)
        for at in range(per_block):
            kept = kept + jnp.where(place == at, 1.0, 0.0) * summed[:, at * width:(at + 1) * width]
        out_ref[...] = kept

    for copy in sends:
        copy.wait_send()
    for off in range(1, n_space):
        share_copy(off).wait_send()

    @pl.when(has_before)
    def _():
        for copy in edge_copies(0):
            copy.wait_send()

    @pl.when(has_after)
    def _():
        for copy in edge_copies(1):
            copy.wait_send()


def on_device(
    n_space, n_corner,
    design, corner_set, corner_dose, kernel_taps, kernel_weights, support_mask, load_mask, force,
):
    rows, columns = design.shape
    kernels = kernel_taps.shape[2]
    radius = kernel_taps.shape[3] // 2
    span = rows + 2 * EDGE
    reach = rows + 2 * HALO
    blocks = columns // LANES
    padded_rows = span + 2 * PAD
    in_hbm = pl.BlockSpec(memory_space=pltpu.HBM)
    in_vmem = pl.BlockSpec(memory_space=pltpu.VMEM)
    scratch = [
        pltpu.SMEM(corner_set.shape, jnp.int32),
        pltpu.SMEM(corner_dose.shape, f32),
        pltpu.SMEM(kernel_weights.shape, f32),
        pltpu.SMEM(force.shape, f32),
        pltpu.VMEM(design.shape, f32),
        pltpu.VMEM(kernel_taps.shape, f32),
        pltpu.VMEM(design.shape, jnp.int32),
        pltpu.VMEM(design.shape, jnp.int32),
        pltpu.VMEM((4 * kernels, LANES), f32),
        pltpu.VMEM((4 * kernels, LANES), f32),
        pltpu.VMEM((4 * kernels, LANES), f32),
        pltpu.VMEM((kernels, 4 * LANES, 2 * LANES), bf16),
        pltpu.VMEM((2 * kernels * (LANES + 4 * radius), 2 * LANES), bf16),
        pltpu.VMEM((kernels, 4 * span, 2 * LANES), bf16),
        pltpu.VMEM((kernels, 4 * rows, 2 * LANES), bf16),
        pltpu.VMEM((2 * HALO, columns), f32),
        pltpu.VMEM((2, 2 * MASK_HALO, columns), jnp.int32),
        pltpu.VMEM((blocks * rows, 4 * LANES), bf16),
        pltpu.VMEM((kernels, 2 * reach, columns), bf16),
        pltpu.VMEM((kernels, 2 * reach, columns), bf16),
        pltpu.VMEM((kernels, 2 * span, columns), f32),
        pltpu.VMEM((blocks, rows, 2 * kernels * (LANES + 4 * radius)), bf16),
        pltpu.VMEM((blocks, rows, 2 * kernels * LANES), bf16),
        pltpu.VMEM((blocks, rows, 8 * kernels * radius), f32),
        pltpu.VMEM((span, columns), f32),
        pltpu.VMEM((padded_rows, columns), f32),
        pltpu.VMEM((span, columns), f32),
        pltpu.VMEM((padded_rows, columns), f32),
        pltpu.VMEM((span, columns), f32),
        pltpu.VMEM((padded_rows, columns), f32),
        pltpu.VMEM((padded_rows, columns), f32),
        pltpu.VMEM((padded_rows, columns), f32),
        pltpu.VMEM((span, columns), f32),
        pltpu.VMEM((span, columns), f32),
        pltpu.VMEM((blocks, rows, LANES), f32),
        pltpu.VMEM((8, LANES), f32),
        pltpu.VMEM((n_space - 1, 8, LANES), f32),
        pltpu.VMEM((n_corner - 1, rows, LANES), f32),
        pltpu.SemaphoreType.DMA((8,)),
        pltpu.SemaphoreType.DMA((2, 3)),
        pltpu.SemaphoreType.DMA((2, 3)),
        pltpu.SemaphoreType.DMA((n_space - 1,)),
        pltpu.SemaphoreType.DMA((n_space - 1,)),
        pltpu.SemaphoreType.DMA((n_corner - 1,)),
        pltpu.SemaphoreType.DMA((n_corner - 1,)),
    ]
    return pl.pallas_call(
        functools.partial(kernel, n_space, n_corner, kernels, radius),
        out_shape=jax.ShapeDtypeStruct((rows, columns // n_corner), f32),
        in_specs=[in_hbm] * 8,
        out_specs=in_vmem,
        scratch_shapes=scratch,
        compiler_params=pltpu.CompilerParams(
            collective_id=0, has_side_effects=True, vmem_limit_bytes=56 * 1024 * 1024
        ),
    )(
        corner_set, corner_dose, kernel_weights, force,
        design, kernel_taps, support_mask, load_mask,
    )


def solution(mesh):
    placed = (
        P("space", None),
        P("corner"),
        P("corner"),
        P(),
        P(),
        P("space", None),
        P("space", None),
        P(),
    )
    body = functools.partial(on_device, mesh.shape["space"], mesh.shape["corner"])
    return jax.shard_map(
        body, mesh=mesh, in_specs=placed, out_specs=P("space", "corner"), check_vma=False
    )
```

```python
import functools
import math

import jax
import jax.numpy as jnp
from jax import lax
from jax.experimental import pallas as pl
from jax.experimental.pallas import tpu as pltpu
from jax.sharding import PartitionSpec as P

MESH = pl.DeviceIdType.MESH
LANES = 128
HALO = 24
MASK_HALO = 16
EDGE = 12
PAD = 8

beta_sharp = 8.0
eta_level = 0.25
stiff_floor = 0.05
kappa_ground = 0.1
shear = 0.35
bf16 = jnp.bfloat16
f32 = jnp.float32


def halves(value):
    high = value.astype(bf16)
    return high, (value - high.astype(f32)).astype(bf16)


def dot(left, right):
    return jnp.dot(left, right, preferred_element_type=f32)


def circulant(row, count, shift):
    turned = pltpu.roll(jnp.broadcast_to(row, (8, LANES)), shift, 1) if shift else row
    return pltpu.roll(
        jnp.broadcast_to(turned[:1], (count, LANES)), 0, 1, stride=1, stride_axis=0
    )


def side_lanes(blocks, at):
    zero = jnp.zeros_like(blocks[0])
    before = blocks[at - 1] if at > 0 else zero
    after = blocks[at + 1] if at + 1 < len(blocks) else zero
    lane = lax.broadcasted_iota(jnp.int32, zero.shape, 1)
    return jnp.where(lane < LANES // 2, after, before)


def kernel(
    n_space, n_corner, kernels, radius,
    set_any, dose_any, weight_any, force_any, design_any, taps_any, support_any, load_any,
    out_ref,
    set_ref, dose_ref, weight_ref, force_ref, design_ref, taps_ref, support_ref, load_ref,
    tap_rows, base_plain, base_flip,
    col_all, back_col, row_both, back_row_both,
    halo, mask_halo, left_all, mid_hi, mid_lo, fields, back_hi, back_lo, sides_held, bright,
    stiff, ground, face_dn, face_rt, loads, image0, image1, factor, gain,
    term, share, shares, landed,
    local_sem, halo_send, halo_recv, share_send, share_recv, term_send, term_recv,
):
    local = [
        pltpu.make_async_copy(source, target, local_sem.at[at])
        for at, (source, target) in enumerate((
            (taps_any, taps_ref), (set_any, set_ref), (dose_any, dose_ref), (weight_any, weight_ref),
            (force_any, force_ref), (design_any, design_ref), (load_any, load_ref), (support_any, support_ref),
        ))
    ]
    for copy in local:
        copy.start()
    rows, columns = design_ref.shape
    span = rows + 2 * EDGE
    blocks = columns // LANES
    strips = span // 8
    me_s = lax.axis_index("space")
    me_c = lax.axis_index("corner")

    barrier = pltpu.get_barrier_semaphore()
    for off in range(1, n_space):
        pl.semaphore_signal(
            barrier, inc=1, device_id={"space": lax.rem(me_s + off, n_space)}, device_id_type=MESH
        )
    for off in range(1, n_corner):
        pl.semaphore_signal(
            barrier, inc=1, device_id={"corner": lax.rem(me_c + off, n_corner)}, device_id_type=MESH
        )

    pl.semaphore_wait(barrier, n_space + n_corner - 2)

    def edge_copies(toward):
        other = lax.rem(me_s + (n_space - 1 if toward == 0 else 1), n_space)
        sent = []
        for which_one, (source, target, width) in enumerate((
            (design_any, halo, HALO),
            (load_any, mask_halo.at[0], MASK_HALO),
            (support_any, mask_halo.at[1], MASK_HALO),
        )):
            begin = 0 if toward == 0 else rows - width
            sent.append(pltpu.make_async_remote_copy(
                src_ref=source.at[pl.ds(begin, width)],
                dst_ref=target.at[pl.ds(toward * width, width)],
                send_sem=halo_send.at[toward, which_one],
                recv_sem=halo_recv.at[toward, which_one],
                device_id={"space": other},
                device_id_type=MESH,
            ))
        return sent

    has_before = me_s > 0
    has_after = me_s < n_space - 1

    @pl.when(has_before)
    def _():
        for copy in edge_copies(0):
            copy.start()

    @pl.when(has_after)
    def _():
        for copy in edge_copies(1):
            copy.start()

    for copy in local[:5]:
        copy.wait()

    chosen = set_ref[0]
    tap_rows[...] = jnp.zeros_like(tap_rows)
    for part in range(4):
        tap_rows[pl.ds(part * kernels, kernels), pl.ds(0, 2 * radius + 1)] = taps_ref[chosen, part]
    table = tap_rows[...]
    base_plain[...] = pltpu.roll(table, LANES - radius, 1)
    from_lane = lax.broadcasted_iota(jnp.int32, (LANES, LANES), 0)
    to_lane = lax.broadcasted_iota(jnp.int32, (LANES, LANES), 1)
    mirror = ((from_lane + to_lane) % LANES == radius).astype(f32)
    base_flip[...] = jnp.dot(
        table, mirror, preferred_element_type=f32, precision=lax.Precision.HIGHEST
    )
    sums = jnp.sum(table, axis=1, keepdims=True)
    sums = [sums[part * kernels:(part + 1) * kernels] for part in range(4)]
    which = lax.broadcasted_iota(jnp.int32, (kernels, 1), 0)
    weight_col = jnp.zeros((kernels, 1), f32)
    for at in range(kernels):
        weight_col = jnp.where(which == at, weight_ref[chosen, at], weight_col)
    clear = jnp.sum(
        weight_col
        * (sums[0] * sums[0] + sums[1] * sums[1])
        * (sums[2] * sums[2] + sums[3] * sums[3]),
        axis=0, keepdims=True,
    )
    dose = dose_ref[0]

    near = jnp.abs(from_lane - to_lane) <= radius
    lane_row = lax.broadcasted_iota(jnp.int32, (span, LANES), 1)
    lane_out = lax.broadcasted_iota(jnp.int32, (rows, LANES), 1)
    reach = rows + 2 * HALO

    def build(at, carry):
        def plain(part):
            return base_plain[pl.ds(part * kernels + at, 1), :]

        def flip(part):
            return base_flip[pl.ds(part * kernels + at, 1), :]

        for part in range(2):
            there = pl.ds(part * LANES, LANES)
            band = circulant(plain(2 + part), LANES, 0)
            hi = band.astype(bf16).astype(f32)
            lo = band - hi
            far_hi = jnp.where(near, 0.0, hi)
            far_lo = jnp.where(near, 0.0, lo)
            near_hi = jnp.where(near, hi, 0.0).astype(bf16)
            col_all[at, pl.ds(0, LANES), there] = near_hi
            col_all[at, pl.ds(LANES, LANES), there] = near_hi
            col_all[at, pl.ds(2 * LANES, LANES), there] = jnp.where(near, lo, 0.0).astype(bf16)
            col_all[at, pl.ds(3 * LANES, LANES), there] = (
                far_hi + pltpu.roll(far_hi, 2 * radius, 0) + pltpu.roll(far_lo, 4 * radius, 0)
            ).astype(bf16)
            band = circulant(flip(2 + part), LANES, 0)
            hi = band.astype(bf16).astype(f32)
            lo = band - hi
            field = 2 * at + part
            begin = pl.multiple_of(field * LANES, LANES)
            back_col[pl.ds(begin, LANES), pl.ds(0, LANES)] = jnp.where(near, hi, 0.0).astype(bf16)
            back_col[pl.ds(begin, LANES), pl.ds(LANES, LANES)] = jnp.where(near, lo, 0.0).astype(bf16)
            far = jnp.concatenate([jnp.where(near, 0.0, hi), jnp.where(near, 0.0, lo)], axis=1)
            far = jnp.concatenate([far[LANES - radius:], far[:radius]], axis=0)
            begin = pl.multiple_of(2 * kernels * LANES + field * 2 * radius, 2 * radius)
            back_col[pl.ds(begin, 2 * radius), :] = far.astype(bf16)
            back_col[pl.ds(begin + 4 * kernels * radius, 2 * radius), pl.ds(0, LANES)] = (
                far[:, :LANES].astype(bf16)
            )
            back_col[pl.ds(begin + 4 * kernels * radius, 2 * radius), pl.ds(LANES, LANES)] = (
                jnp.zeros((2 * radius, LANES), bf16)
            )

        def joined(first, second, lane, width):
            turned = pltpu.roll(second, width, 1)
            left = jnp.where(lane < width, first, turned)
            right = jnp.where(lane < 2 * width - LANES, turned, 0.0)
            return jnp.concatenate([left, right], axis=1)

        def forward_rows(part):
            band = circulant(flip(part), span, LANES - EDGE)
            band = jnp.where(lane_row < rows + HALO, band, pltpu.roll(band, reach, 1))
            return jnp.where(lane_row < reach, band, 0.0)

        row_re = forward_rows(0)
        row_im = forward_rows(1)
        matrix = jnp.concatenate(
            [joined(row_re, -row_im, lane_row, reach), joined(row_im, row_re, lane_row, reach)], axis=0
        )
        hi, lo = halves(matrix)
        row_both[at, pl.ds(0, 2 * span), :] = hi
        row_both[at, pl.ds(2 * span, 2 * span), :] = lo
        scale = 2.0 * weight_ref[chosen, at]
        row_re = circulant(plain(0), rows, EDGE) * scale
        row_im = circulant(plain(1), rows, EDGE) * scale
        matrix = jnp.concatenate(
            [joined(row_re, -row_im, lane_out, span), joined(-row_im, -row_re, lane_out, span)], axis=0
        )
        hi, lo = halves(matrix)
        back_row_both[at, pl.ds(0, 2 * rows), :] = hi
        back_row_both[at, pl.ds(2 * rows, 2 * rows), :] = lo
        return carry

    lax.fori_loop(0, kernels, build, 0)

    def columns_of(cells, begin):
        parts = [cells[:, at * LANES:(at + 1) * LANES] for at in range(blocks)]
        for at in range(blocks):
            hi, lo = halves(parts[at])
            side = side_lanes(parts, at)
            side_hi = side.astype(bf16).astype(f32)
            packed = jnp.where(
                (lane_out < radius) | (lane_out >= LANES - radius),
                side_hi,
                jnp.where(
                    lane_out < 3 * radius,
                    pltpu.roll(side - side_hi, 2 * radius, 1),
                    jnp.where(lane_out < 5 * radius, pltpu.roll(side_hi, 4 * radius, 1), 0.0),
                ),
            )
            left_all[pl.ds(at * rows, rows), :] = jnp.concatenate([hi, lo, hi, packed.astype(bf16)], axis=1)

        for at in range(kernels):
            value = dot(left_all[...], col_all[at])
            hi, lo = halves(value)
            for block in range(blocks):
                for part in range(2):
                    here = (slice(block * rows, (block + 1) * rows), slice(part * LANES, (part + 1) * LANES))
                    there = (at, pl.ds(part * reach + begin, rows), pl.ds(block * LANES, LANES))
                    mid_hi[there] = hi[here]
                    mid_lo[there] = lo[here]

    local[5].wait()
    columns_of(design_ref[...], 0)

    @pl.when(has_after)
    def _():
        for copy in edge_copies(0):
            copy.wait_recv()

    @pl.when(jnp.logical_not(has_after))
    def _():
        halo[pl.ds(0, HALO), :] = jnp.zeros((HALO, columns), f32)
        mask_halo[:, pl.ds(0, MASK_HALO), :] = jnp.zeros((2, MASK_HALO, columns), jnp.int32)

    @pl.when(has_before)
    def _():
        for copy in edge_copies(1):
            copy.wait_recv()

    @pl.when(jnp.logical_not(has_before))
    def _():
        halo[pl.ds(HALO, HALO), :] = jnp.zeros((HALO, columns), f32)
        mask_halo[:, pl.ds(MASK_HALO, MASK_HALO), :] = jnp.zeros((2, MASK_HALO, columns), jnp.int32)

    columns_of(halo[...], rows)

    for at in range(kernels):
        both = row_both[at][:, :2 * reach]
        of_high = dot(both, mid_hi[at])
        value = of_high[:2 * span] + of_high[2 * span:] + dot(both[:2 * span], mid_lo[at])
        fields[at] = value
        light = weight_ref[chosen, at] * (value[:span] * value[:span] + value[span:] * value[span:])
        bright[...] = light if at == 0 else bright[...] + light

    for copy in local[6:]:
        copy.wait()

    zero_pad = jnp.zeros((PAD, columns), f32)
    for array in (stiff, loads, image0, image1):
        array[pl.ds(0, PAD), :] = zero_pad
        array[pl.ds(PAD + span, PAD), :] = zero_pad
    for which_one, own, target, base in ((0, load_ref, loads, PAD), (1, support_ref, ground, 0)):
        target[pl.ds(base, EDGE), :] = mask_halo[which_one, pl.ds(2 * MASK_HALO - EDGE, EDGE), :].astype(f32)
        target[pl.ds(base + EDGE, rows), :] = own[...].astype(f32)
        target[pl.ds(base + EDGE + rows, EDGE), :] = mask_halo[which_one, pl.ds(0, EDGE), :].astype(f32)

    row_in = lax.broadcasted_iota(jnp.int32, (8, columns), 0)
    lane_in = lax.broadcasted_iota(jnp.int32, (8, columns), 1)
    first_row = me_s * rows - EDGE
    grid_rows = n_space * rows
    low_end = math.tanh(beta_sharp * eta_level)
    spread = low_end + math.tanh(beta_sharp * (1.0 - eta_level))
    level = dose / clear
    gain_scale = level * (3.0 * (1.0 - stiff_floor) * beta_sharp / spread)

    def strip_of(strip):
        return pl.multiple_of(strip * 8, 8)

    def project(strip, carry):
        begin = strip_of(strip)
        light = bright[pl.ds(begin, 8), :] * level
        bent = jnp.tanh(beta_sharp * (light - eta_level))
        density = (low_end + bent) * (1.0 / spread)
        square = density * density
        grid_row = row_in + (first_row + begin)
        inside = (grid_row >= 0) & (grid_row < grid_rows)
        hard = jnp.where(inside, stiff_floor + (1.0 - stiff_floor) * square * density, 0.0)
        stiff[pl.ds(begin + PAD, 8), :] = hard
        ground[pl.ds(begin, 8), :] = kappa_ground * hard + ground[pl.ds(begin, 8), :]
        factor[pl.ds(begin, 8), :] = jnp.where(
            inside, -gain_scale * square * (1.0 - bent * bent), 0.0
        )
        return carry

    lax.fori_loop(0, strips, project, 0)

    force0 = force_ref[0]
    force1 = force_ref[1]

    def two(array, strip):
        begin = strip_of(strip)
        return array[pl.ds(begin + PAD, 8), :], array[pl.ds(begin + PAD + 8, 8), :]

    def row_below(here, after):
        return jnp.where(row_in == 7, pltpu.roll(after, 7, 0), pltpu.roll(here, 7, 0))

    def row_above(here, before):
        return jnp.where(row_in == 0, pltpu.roll(before, 1, 0), pltpu.roll(here, 1, 0))

    def on_right(here):
        return pltpu.roll(here, columns - 1, 1)

    def on_left(here):
        return pltpu.roll(here, 1, 1)

    def own_rows(strip):
        row = row_in + strip_of(strip)
        return (row >= EDGE) & (row < EDGE + rows)

    def folded(cells):
        return sum(cells[:, block * LANES:(block + 1) * LANES] for block in range(blocks))

    blank = jnp.zeros((8, columns), f32)
    narrow = jnp.zeros((8, LANES), f32)

    def first_image(strip, carry):
        flux_before, norm, energy = carry
        begin = strip_of(strip)
        hard, hard_after = two(stiff, strip)
        hard_below = row_below(hard, hard_after)
        hard_right = on_right(hard)
        face_down = 2.0 * hard * hard_below / jnp.maximum(hard + hard_below, 1e-20)
        face_right = 2.0 * hard * hard_right / jnp.maximum(hard + hard_right, 1e-20)
        face_right = jnp.where(lane_in < columns - 1, face_right, 0.0)
        face_dn[pl.ds(begin, 8), :] = face_down
        face_rt[pl.ds(begin, 8), :] = face_right
        here, after = two(loads, strip)
        flux = face_down * (here - row_below(here, after))
        along_rows = flux - row_above(flux, flux_before)
        across = face_right * (here - on_right(here))
        along_columns = across - on_left(across)
        held = ground[pl.ds(begin, 8), :] * here
        one = force0 * (held + along_rows + shear * along_columns)
        other = force1 * (held + shear * along_rows + along_columns)
        image0[pl.ds(begin + PAD, 8), :] = one
        image1[pl.ds(begin + PAD, 8), :] = other
        own = jnp.where(own_rows(strip), here, 0.0)
        return flux, norm + folded(own * own), energy + folded(own * (force0 * one + force1 * other))

    flux, norm, energy = lax.fori_loop(0, strips, first_image, (blank, narrow, narrow))

    def whole_sum(cells):
        return jnp.sum(jnp.sum(cells, axis=0, keepdims=True), axis=1, keepdims=True)

    norm = whole_sum(norm) * (force0 * force0 + force1 * force1)
    energy = whole_sum(energy)
    ratio = jnp.where(norm > 0.0, energy / jnp.where(norm > 0.0, norm, 1.0), 0.0)

    def second_image(strip, carry):
        flux_before, sums = list(carry[:2]), list(carry[2:])
        begin = strip_of(strip)
        face_down = face_dn[pl.ds(begin, 8), :]
        face_right = face_rt[pl.ds(begin, 8), :]
        load, load_after = two(loads, strip)
        held = ground[pl.ds(begin, 8), :]
        keep = own_rows(strip)
        for at, (array, push, of_rows, of_columns) in enumerate((
            (image0, force0, 1.0, shear), (image1, force1, shear, 1.0)
        )):
            image, image_after = two(array, strip)
            lean = ratio * push
            here = image - lean * load
            flux = face_down * (here - row_below(here, image_after - lean * load_after))
            along_rows = flux - row_above(flux, flux_before[at])
            flux_before[at] = flux
            across = face_right * (here - on_right(here))
            along_columns = across - on_left(across)
            applied = held * here + of_rows * along_rows + of_columns * along_columns
            applied = jnp.where(keep, applied, 0.0)
            sums[0] = sums[0] + folded(jnp.where(keep, here * here, 0.0))
            sums[1] = sums[1] + folded(here * applied)
            sums[2] = sums[2] + push * folded(load * applied)
        return tuple(flux_before + sums)

    first_strip = EDGE // 8
    last_strip = (EDGE + rows + 7) // 8
    rest = lax.fori_loop(
        first_strip, last_strip, second_image, (blank, blank, narrow, narrow, narrow)
    )[2:]
    values = [norm, ratio] + [whole_sum(cells) for cells in rest]
    lane8 = lax.broadcasted_iota(jnp.int32, (8, LANES), 1)
    packed = jnp.zeros((8, LANES), f32)
    for at, value in enumerate(values):
        packed = jnp.where(lane8 == at, value, packed)
    share[...] = packed

    def share_copy(off):
        return pltpu.make_async_remote_copy(
            src_ref=share,
            dst_ref=shares.at[off - 1],
            send_sem=share_send.at[off - 1],
            recv_sem=share_recv.at[off - 1],
            device_id={"space": lax.rem(me_s + off, n_space)},
            device_id_type=MESH,
        )

    for off in range(1, n_space):
        share_copy(off).start()
    for off in range(1, n_space):
        share_copy(off).wait_recv()
    tables = [packed] + [shares[off - 1] for off in range(1, n_space)]
    lists = [[each[0:1, at:at + 1] for at in range(5)] for each in tables]
    norm_now = sum(each[0] for each in lists)
    centre = sum(each[0] * each[1] for each in lists) / norm_now
    spare = 0.0
    bend = 0.0
    for part_norm, part_ratio, part_spare, part_bend, part_cross in lists:
        shift = part_ratio - centre
        spare = spare + part_spare + shift * shift * part_norm
        bend = bend + part_bend + shift * (part_cross + part_spare) + shift * shift * part_ratio * part_norm
    inverse = 1.0 / centre
    norm_next = spare * inverse * inverse
    renew = norm_next / norm_now
    curve = bend * inverse * inverse - renew * norm_next * centre
    step = norm_next / curve
    of_load = inverse + step * (1.0 + renew)
    of_image = -step * inverse

    def slopes(strip, bend_before):
        begin = strip_of(strip)
        face_down = face_dn[pl.ds(begin, 8), :]
        face_right = face_rt[pl.ds(begin, 8), :]
        load, load_after = two(loads, strip)
        hard = stiff[pl.ds(begin + PAD, 8), :]
        held = jnp.zeros((8, columns), f32)
        bend_down = jnp.zeros((8, columns), f32)
        bend_right = jnp.zeros((8, columns), f32)
        for array, push, of_rows, of_columns in (
            (image0, force0, 1.0, shear), (image1, force1, shear, 1.0)
        ):
            image, image_after = two(array, strip)
            lean = of_load * push
            here = lean * load + of_image * image
            down = here - row_below(here, lean * load_after + of_image * image_after)
            right = here - on_right(here)
            held = held + here * here
            bend_down = bend_down + of_rows * (down * down)
            bend_right = bend_right + of_columns * (right * right)
        bend_down = face_down * face_down * bend_down
        bend_right = face_right * face_right * bend_right
        bent = bend_down + row_above(bend_down, bend_before) + bend_right + on_left(bend_right)
        bent = bent * 0.5 / jnp.maximum(hard * hard, 1e-6)
        gain[pl.ds(begin, 8), :] = factor[pl.ds(begin, 8), :] * (kappa_ground * held + bent)
        return bend_down

    lax.fori_loop(0, strips, slopes, blank)

    for at in range(kernels):
        scale = gain[...]
        sent = jnp.concatenate(
            [fields[at, pl.ds(0, span), :] * scale, -(fields[at, pl.ds(span, span), :] * scale)], axis=0
        )
        hi, lo = halves(sent)
        both = back_row_both[at][:, :2 * span]
        of_high = dot(both, hi)
        turned = of_high[:2 * rows] + of_high[2 * rows:] + dot(both[:2 * rows], lo)
        for part in range(2):
            piece = turned[part * rows:(part + 1) * rows]
            parts = [piece[:, block * LANES:(block + 1) * LANES] for block in range(blocks)]
            for block in range(blocks):
                field = 2 * at + part
                hi, lo = halves(parts[block])
                lanes = pl.ds(field * LANES, LANES)
                back_hi[block, :, lanes] = hi
                back_lo[block, :, lanes] = lo
                edge = side_lanes(parts, block)
                edge_hi = edge.astype(bf16).astype(f32)
                slots = LANES // (2 * radius)
                place = field % slots
                turn = radius + place * 2 * radius
                keep = lane_out // (2 * radius) == place
                for group, cells in ((field // slots, edge_hi), (2 * kernels // slots + field // slots, edge - edge_hi)):
                    moved = pltpu.roll(cells, turn % LANES, 1)
                    lanes = pl.ds(group * LANES, LANES)
                    moved = jnp.where(keep, moved, 0.0 if place == 0 else sides_held[block, :, lanes])
                    if place == slots - 1:
                        lanes = pl.ds((2 * kernels + group) * LANES, LANES)
                        back_hi[block, :, lanes] = moved.astype(bf16)
                    else:
                        sides_held[block, :, lanes] = moved

    width = columns // n_corner
    per_block = LANES // width
    my_block = me_c // per_block

    def term_copy(block, other, sent_as):
        slot = lax.rem(other - me_c + n_corner, n_corner) - 1
        return pltpu.make_async_remote_copy(
            src_ref=term.at[block],
            dst_ref=landed.at[slot],
            send_sem=term_send.at[sent_as],
            recv_sem=term_recv.at[slot],
            device_id={"corner": other},
            device_id_type=MESH,
        )

    sends = []
    half = blocks // 2
    ahead = [half, half - 1, half + 1, half + 2] + [at for at in range(half - 2, 0, -1)]
    ahead += [at for at in range(half + 3, blocks)] + [0]
    for group in (ahead[:half], ahead[half:]):
        places = [lax.rem(my_block + at, blocks) for at in group]
        hi = jnp.concatenate([back_hi[place] for place in places], axis=0)
        lo = jnp.concatenate([back_lo[place] for place in places], axis=0)
        wide = dot(hi, back_col[...])
        value = wide[:, :LANES] + wide[:, LANES:] + dot(lo, back_col[pl.ds(0, 2 * kernels * LANES), pl.ds(0, LANES)])
        for at, place in enumerate(places):
            term[place] = value[at * rows:(at + 1) * rows]
        for at, place in zip(group, places):
            for step in range(per_block):
                if at == 0 and step == 0:
                    continue
                other = place * per_block + lax.rem(me_c + step, per_block)
                copy = term_copy(place, other, len(sends))
                copy.start()
                sends.append(copy)
    summed = term[my_block]
    for off in range(1, n_corner):
        term_copy(my_block, lax.rem(me_c + off, n_corner), off - 1).wait_recv()
        summed = summed + landed[off - 1]
    if per_block == 1:
        out_ref[...] = summed
    else:
        place = lax.rem(me_c, per_block)
        kept = jnp.zeros(out_ref.shape, f32)
        for at in range(per_block):
            kept = kept + jnp.where(place == at, 1.0, 0.0) * summed[:, at * width:(at + 1) * width]
        out_ref[...] = kept

    for copy in sends:
        copy.wait_send()
    for off in range(1, n_space):
        share_copy(off).wait_send()

    @pl.when(has_before)
    def _():
        for copy in edge_copies(0):
            copy.wait_send()

    @pl.when(has_after)
    def _():
        for copy in edge_copies(1):
            copy.wait_send()


def on_device(
    n_space, n_corner,
    design, corner_set, corner_dose, kernel_taps, kernel_weights, support_mask, load_mask, force,
):
    rows, columns = design.shape
    kernels = kernel_taps.shape[2]
    radius = kernel_taps.shape[3] // 2
    span = rows + 2 * EDGE
    reach = rows + 2 * HALO
    blocks = columns // LANES
    padded_rows = span + 2 * PAD
    in_hbm = pl.BlockSpec(memory_space=pltpu.HBM)
    in_vmem = pl.BlockSpec(memory_space=pltpu.VMEM)
    scratch = [
        pltpu.SMEM(corner_set.shape, jnp.int32),
        pltpu.SMEM(corner_dose.shape, f32),
        pltpu.SMEM(kernel_weights.shape, f32),
        pltpu.SMEM(force.shape, f32),
        pltpu.VMEM(design.shape, f32),
        pltpu.VMEM(kernel_taps.shape, f32),
        pltpu.VMEM(design.shape, jnp.int32),
        pltpu.VMEM(design.shape, jnp.int32),
        pltpu.VMEM((4 * kernels, LANES), f32),
        pltpu.VMEM((4 * kernels, LANES), f32),
        pltpu.VMEM((4 * kernels, LANES), f32),
        pltpu.VMEM((kernels, 4 * LANES, 2 * LANES), bf16),
        pltpu.VMEM((2 * kernels * (LANES + 4 * radius), 2 * LANES), bf16),
        pltpu.VMEM((kernels, 4 * span, 2 * LANES), bf16),
        pltpu.VMEM((kernels, 4 * rows, 2 * LANES), bf16),
        pltpu.VMEM((2 * HALO, columns), f32),
        pltpu.VMEM((2, 2 * MASK_HALO, columns), jnp.int32),
        pltpu.VMEM((blocks * rows, 4 * LANES), bf16),
        pltpu.VMEM((kernels, 2 * reach, columns), bf16),
        pltpu.VMEM((kernels, 2 * reach, columns), bf16),
        pltpu.VMEM((kernels, 2 * span, columns), f32),
        pltpu.VMEM((blocks, rows, 2 * kernels * (LANES + 4 * radius)), bf16),
        pltpu.VMEM((blocks, rows, 2 * kernels * LANES), bf16),
        pltpu.VMEM((blocks, rows, 8 * kernels * radius), f32),
        pltpu.VMEM((span, columns), f32),
        pltpu.VMEM((padded_rows, columns), f32),
        pltpu.VMEM((span, columns), f32),
        pltpu.VMEM((padded_rows, columns), f32),
        pltpu.VMEM((span, columns), f32),
        pltpu.VMEM((padded_rows, columns), f32),
        pltpu.VMEM((padded_rows, columns), f32),
        pltpu.VMEM((padded_rows, columns), f32),
        pltpu.VMEM((span, columns), f32),
        pltpu.VMEM((span, columns), f32),
        pltpu.VMEM((blocks, rows, LANES), f32),
        pltpu.VMEM((8, LANES), f32),
        pltpu.VMEM((n_space - 1, 8, LANES), f32),
        pltpu.VMEM((n_corner - 1, rows, LANES), f32),
        pltpu.SemaphoreType.DMA((8,)),
        pltpu.SemaphoreType.DMA((2, 3)),
        pltpu.SemaphoreType.DMA((2, 3)),
        pltpu.SemaphoreType.DMA((n_space - 1,)),
        pltpu.SemaphoreType.DMA((n_space - 1,)),
        pltpu.SemaphoreType.DMA((n_corner - 1,)),
        pltpu.SemaphoreType.DMA((n_corner - 1,)),
    ]
    return pl.pallas_call(
        functools.partial(kernel, n_space, n_corner, kernels, radius),
        out_shape=jax.ShapeDtypeStruct((rows, columns // n_corner), f32),
        in_specs=[in_hbm] * 8,
        out_specs=in_vmem,
        scratch_shapes=scratch,
        compiler_params=pltpu.CompilerParams(
            collective_id=0, has_side_effects=True, vmem_limit_bytes=56 * 1024 * 1024
        ),
    )(
        corner_set, corner_dose, kernel_weights, force,
        design, kernel_taps, support_mask, load_mask,
    )


def solution(mesh):
    placed = (
        P("space", None),
        P("corner"),
        P("corner"),
        P(),
        P(),
        P("space", None),
        P("space", None),
        P(),
    )
    body = functools.partial(on_device, mesh.shape["space"], mesh.shape["corner"])
    return jax.shard_map(
        body, mesh=mesh, in_specs=placed, out_specs=P("space", "corner"), check_vma=False
    )
```

```python
import functools
import math

import jax
import jax.numpy as jnp
from jax import lax
from jax.experimental import pallas as pl
from jax.experimental.pallas import tpu as pltpu
from jax.sharding import PartitionSpec as P

MESH = pl.DeviceIdType.MESH
LANES = 128
HALO = 24
MASK_HALO = 16
EDGE = 12
PAD = 8

beta_sharp = 8.0
eta_level = 0.25
stiff_floor = 0.05
kappa_ground = 0.1
shear = 0.35
bf16 = jnp.bfloat16
f32 = jnp.float32


def halves(value):
    high = value.astype(bf16)
    return high, (value - high.astype(f32)).astype(bf16)


def dot(left, right):
    return jnp.dot(left, right, preferred_element_type=f32)


def circulant(row, count, shift):
    turned = pltpu.roll(jnp.broadcast_to(row, (8, LANES)), shift, 1) if shift else row
    return pltpu.roll(
        jnp.broadcast_to(turned[:1], (count, LANES)), 0, 1, stride=1, stride_axis=0
    )


def side_lanes(blocks, at):
    zero = jnp.zeros_like(blocks[0])
    before = blocks[at - 1] if at > 0 else zero
    after = blocks[at + 1] if at + 1 < len(blocks) else zero
    lane = lax.broadcasted_iota(jnp.int32, zero.shape, 1)
    return jnp.where(lane < LANES // 2, after, before)


def kernel(
    n_space, n_corner, kernels, radius,
    set_any, dose_any, weight_any, force_any, design_any, taps_any, support_any, load_any,
    out_ref,
    set_ref, dose_ref, weight_ref, force_ref, design_ref, taps_ref, support_ref, load_ref,
    tap_rows, base_plain, base_flip,
    col_all, back_col, row_both, back_row_both,
    halo, mask_halo, left_all, mid_hi, mid_lo, fields, back_hi, back_lo, sides_held, bright,
    stiff, ground, face_dn, face_rt, loads, image0, image1, factor, gain,
    term, share, shares, landed,
    local_sem, halo_send, halo_recv, share_send, share_recv, term_send, term_recv,
):
    local = [
        pltpu.make_async_copy(source, target, local_sem.at[at])
        for at, (source, target) in enumerate((
            (taps_any, taps_ref), (set_any, set_ref), (dose_any, dose_ref), (weight_any, weight_ref),
            (force_any, force_ref), (design_any, design_ref), (load_any, load_ref), (support_any, support_ref),
        ))
    ]
    for copy in local:
        copy.start()
    rows, columns = design_ref.shape
    span = rows + 2 * EDGE
    blocks = columns // LANES
    strips = span // 8
    me_s = lax.axis_index("space")
    me_c = lax.axis_index("corner")

    barrier = pltpu.get_barrier_semaphore()
    for off in range(1, n_space):
        pl.semaphore_signal(
            barrier, inc=1, device_id={"space": lax.rem(me_s + off, n_space)}, device_id_type=MESH
        )
    for off in range(1, n_corner):
        pl.semaphore_signal(
            barrier, inc=1, device_id={"corner": lax.rem(me_c + off, n_corner)}, device_id_type=MESH
        )

    pl.semaphore_wait(barrier, n_space + n_corner - 2)

    def edge_copies(toward):
        other = lax.rem(me_s + (n_space - 1 if toward == 0 else 1), n_space)
        sent = []
        for which_one, (source, target, width) in enumerate((
            (design_any, halo, HALO),
            (load_any, mask_halo.at[0], MASK_HALO),
            (support_any, mask_halo.at[1], MASK_HALO),
        )):
            begin = 0 if toward == 0 else rows - width
            sent.append(pltpu.make_async_remote_copy(
                src_ref=source.at[pl.ds(begin, width)],
                dst_ref=target.at[pl.ds(toward * width, width)],
                send_sem=halo_send.at[toward, which_one],
                recv_sem=halo_recv.at[toward, which_one],
                device_id={"space": other},
                device_id_type=MESH,
            ))
        return sent

    has_before = me_s > 0
    has_after = me_s < n_space - 1

    @pl.when(has_before)
    def _():
        for copy in edge_copies(0):
            copy.start()

    @pl.when(has_after)
    def _():
        for copy in edge_copies(1):
            copy.start()

    for copy in local[:5]:
        copy.wait()

    chosen = set_ref[0]
    tap_rows[...] = jnp.zeros_like(tap_rows)
    for part in range(4):
        tap_rows[pl.ds(part * kernels, kernels), pl.ds(0, 2 * radius + 1)] = taps_ref[chosen, part]
    table = tap_rows[...]
    base_plain[...] = pltpu.roll(table, LANES - radius, 1)
    from_lane = lax.broadcasted_iota(jnp.int32, (LANES, LANES), 0)
    to_lane = lax.broadcasted_iota(jnp.int32, (LANES, LANES), 1)
    mirror = ((from_lane + to_lane) % LANES == radius).astype(f32)
    base_flip[...] = jnp.dot(
        table, mirror, preferred_element_type=f32, precision=lax.Precision.HIGHEST
    )
    sums = jnp.sum(table, axis=1, keepdims=True)
    sums = [sums[part * kernels:(part + 1) * kernels] for part in range(4)]
    which = lax.broadcasted_iota(jnp.int32, (kernels, 1), 0)
    weight_col = jnp.zeros((kernels, 1), f32)
    for at in range(kernels):
        weight_col = jnp.where(which == at, weight_ref[chosen, at], weight_col)
    clear = jnp.sum(
        weight_col
        * (sums[0] * sums[0] + sums[1] * sums[1])
        * (sums[2] * sums[2] + sums[3] * sums[3]),
        axis=0, keepdims=True,
    )
    dose = dose_ref[0]

    near = jnp.abs(from_lane - to_lane) <= radius
    lane_row = lax.broadcasted_iota(jnp.int32, (span, LANES), 1)
    lane_out = lax.broadcasted_iota(jnp.int32, (rows, LANES), 1)
    reach = rows + 2 * HALO

    def build(at, carry):
        def plain(part):
            return base_plain[pl.ds(part * kernels + at, 1), :]

        def flip(part):
            return base_flip[pl.ds(part * kernels + at, 1), :]

        for part in range(2):
            there = pl.ds(part * LANES, LANES)
            band = circulant(plain(2 + part), LANES, 0)
            hi = band.astype(bf16).astype(f32)
            lo = band - hi
            far_hi = jnp.where(near, 0.0, hi)
            far_lo = jnp.where(near, 0.0, lo)
            near_hi = jnp.where(near, hi, 0.0).astype(bf16)
            col_all[at, pl.ds(0, LANES), there] = near_hi
            col_all[at, pl.ds(LANES, LANES), there] = near_hi
            col_all[at, pl.ds(2 * LANES, LANES), there] = jnp.where(near, lo, 0.0).astype(bf16)
            col_all[at, pl.ds(3 * LANES, LANES), there] = (
                far_hi + pltpu.roll(far_hi, 2 * radius, 0) + pltpu.roll(far_lo, 4 * radius, 0)
            ).astype(bf16)
            band = circulant(flip(2 + part), LANES, 0)
            hi = band.astype(bf16).astype(f32)
            lo = band - hi
            field = 2 * at + part
            begin = pl.multiple_of(field * LANES, LANES)
            back_col[pl.ds(begin, LANES), pl.ds(0, LANES)] = jnp.where(near, hi, 0.0).astype(bf16)
            back_col[pl.ds(begin, LANES), pl.ds(LANES, LANES)] = jnp.where(near, lo, 0.0).astype(bf16)
            far = jnp.concatenate([jnp.where(near, 0.0, hi), jnp.where(near, 0.0, lo)], axis=1)
            far = jnp.concatenate([far[LANES - radius:], far[:radius]], axis=0)
            begin = pl.multiple_of(2 * kernels * LANES + field * 2 * radius, 2 * radius)
            back_col[pl.ds(begin, 2 * radius), :] = far.astype(bf16)
            back_col[pl.ds(begin + 4 * kernels * radius, 2 * radius), pl.ds(0, LANES)] = (
                far[:, :LANES].astype(bf16)
            )
            back_col[pl.ds(begin + 4 * kernels * radius, 2 * radius), pl.ds(LANES, LANES)] = (
                jnp.zeros((2 * radius, LANES), bf16)
            )

        def joined(first, second, lane, width):
            turned = pltpu.roll(second, width, 1)
            left = jnp.where(lane < width, first, turned)
            right = jnp.where(lane < 2 * width - LANES, turned, 0.0)
            return jnp.concatenate([left, right], axis=1)

        def forward_rows(part):
            band = circulant(flip(part), span, LANES - EDGE)
            band = jnp.where(lane_row < rows + HALO, band, pltpu.roll(band, reach, 1))
            return jnp.where(lane_row < reach, band, 0.0)

        row_re = forward_rows(0)
        row_im = forward_rows(1)
        matrix = jnp.concatenate(
            [joined(row_re, -row_im, lane_row, reach), joined(row_im, row_re, lane_row, reach)], axis=0
        )
        hi, lo = halves(matrix)
        row_both[at, pl.ds(0, 2 * span), :] = hi
        row_both[at, pl.ds(2 * span, 2 * span), :] = lo
        scale = 2.0 * weight_ref[chosen, at]
        row_re = circulant(plain(0), rows, EDGE) * scale
        row_im = circulant(plain(1), rows, EDGE) * scale
        matrix = jnp.concatenate(
            [joined(row_re, -row_im, lane_out, span), joined(-row_im, -row_re, lane_out, span)], axis=0
        )
        hi, lo = halves(matrix)
        back_row_both[at, pl.ds(0, 2 * rows), :] = hi
        back_row_both[at, pl.ds(2 * rows, 2 * rows), :] = lo
        return carry

    lax.fori_loop(0, kernels, build, 0, unroll=True)

    def columns_of(cells, begin):
        parts = [cells[:, at * LANES:(at + 1) * LANES] for at in range(blocks)]
        for at in range(blocks):
            hi, lo = halves(parts[at])
            side = side_lanes(parts, at)
            side_hi = side.astype(bf16).astype(f32)
            packed = jnp.where(
                (lane_out < radius) | (lane_out >= LANES - radius),
                side_hi,
                jnp.where(
                    lane_out < 3 * radius,
                    pltpu.roll(side - side_hi, 2 * radius, 1),
                    jnp.where(lane_out < 5 * radius, pltpu.roll(side_hi, 4 * radius, 1), 0.0),
                ),
            )
            left_all[pl.ds(at * rows, rows), :] = jnp.concatenate([hi, lo, hi, packed.astype(bf16)], axis=1)

        for at in range(kernels):
            value = dot(left_all[...], col_all[at])
            hi, lo = halves(value)
            for block in range(blocks):
                for part in range(2):
                    here = (slice(block * rows, (block + 1) * rows), slice(part * LANES, (part + 1) * LANES))
                    there = (at, pl.ds(part * reach + begin, rows), pl.ds(block * LANES, LANES))
                    mid_hi[there] = hi[here]
                    mid_lo[there] = lo[here]

    local[5].wait()
    columns_of(design_ref[...], 0)

    @pl.when(has_after)
    def _():
        for copy in edge_copies(0):
            copy.wait_recv()

    @pl.when(jnp.logical_not(has_after))
    def _():
        halo[pl.ds(0, HALO), :] = jnp.zeros((HALO, columns), f32)
        mask_halo[:, pl.ds(0, MASK_HALO), :] = jnp.zeros((2, MASK_HALO, columns), jnp.int32)

    @pl.when(has_before)
    def _():
        for copy in edge_copies(1):
            copy.wait_recv()

    @pl.when(jnp.logical_not(has_before))
    def _():
        halo[pl.ds(HALO, HALO), :] = jnp.zeros((HALO, columns), f32)
        mask_halo[:, pl.ds(MASK_HALO, MASK_HALO), :] = jnp.zeros((2, MASK_HALO, columns), jnp.int32)

    columns_of(halo[...], rows)

    for at in range(kernels):
        both = row_both[at][:, :2 * reach]
        of_high = dot(both, mid_hi[at])
        value = of_high[:2 * span] + of_high[2 * span:] + dot(both[:2 * span], mid_lo[at])
        fields[at] = value
        light = weight_ref[chosen, at] * (value[:span] * value[:span] + value[span:] * value[span:])
        bright[...] = light if at == 0 else bright[...] + light

    for copy in local[6:]:
        copy.wait()

    zero_pad = jnp.zeros((PAD, columns), f32)
    for array in (stiff, loads, image0, image1):
        array[pl.ds(0, PAD), :] = zero_pad
        array[pl.ds(PAD + span, PAD), :] = zero_pad
    for which_one, own, target, base in ((0, load_ref, loads, PAD), (1, support_ref, ground, 0)):
        target[pl.ds(base, EDGE), :] = mask_halo[which_one, pl.ds(2 * MASK_HALO - EDGE, EDGE), :].astype(f32)
        target[pl.ds(base + EDGE, rows), :] = own[...].astype(f32)
        target[pl.ds(base + EDGE + rows, EDGE), :] = mask_halo[which_one, pl.ds(0, EDGE), :].astype(f32)

    row_in = lax.broadcasted_iota(jnp.int32, (8, columns), 0)
    lane_in = lax.broadcasted_iota(jnp.int32, (8, columns), 1)
    first_row = me_s * rows - EDGE
    grid_rows = n_space * rows
    low_end = math.tanh(beta_sharp * eta_level)
    spread = low_end + math.tanh(beta_sharp * (1.0 - eta_level))
    level = dose / clear
    gain_scale = level * (3.0 * (1.0 - stiff_floor) * beta_sharp / spread)

    def strip_of(strip):
        return pl.multiple_of(strip * 8, 8)

    def project(strip, carry):
        begin = strip_of(strip)
        light = bright[pl.ds(begin, 8), :] * level
        bent = jnp.tanh(beta_sharp * (light - eta_level))
        density = (low_end + bent) * (1.0 / spread)
        square = density * density
        grid_row = row_in + (first_row + begin)
        inside = (grid_row >= 0) & (grid_row < grid_rows)
        hard = jnp.where(inside, stiff_floor + (1.0 - stiff_floor) * square * density, 0.0)
        stiff[pl.ds(begin + PAD, 8), :] = hard
        ground[pl.ds(begin, 8), :] = kappa_ground * hard + ground[pl.ds(begin, 8), :]
        factor[pl.ds(begin, 8), :] = jnp.where(
            inside, -gain_scale * square * (1.0 - bent * bent), 0.0
        )
        return carry

    lax.fori_loop(0, strips, project, 0, unroll=True)

    force0 = force_ref[0]
    force1 = force_ref[1]

    def two(array, strip):
        begin = strip_of(strip)
        return array[pl.ds(begin + PAD, 8), :], array[pl.ds(begin + PAD + 8, 8), :]

    def row_below(here, after):
        return jnp.where(row_in == 7, pltpu.roll(after, 7, 0), pltpu.roll(here, 7, 0))

    def row_above(here, before):
        return jnp.where(row_in == 0, pltpu.roll(before, 1, 0), pltpu.roll(here, 1, 0))

    def on_right(here):
        return pltpu.roll(here, columns - 1, 1)

    def on_left(here):
        return pltpu.roll(here, 1, 1)

    def own_rows(strip):
        row = row_in + strip_of(strip)
        return (row >= EDGE) & (row < EDGE + rows)

    def folded(cells):
        return sum(cells[:, block * LANES:(block + 1) * LANES] for block in range(blocks))

    blank = jnp.zeros((8, columns), f32)
    narrow = jnp.zeros((8, LANES), f32)

    def first_image(strip, carry):
        flux_before, norm, energy = carry
        begin = strip_of(strip)
        hard, hard_after = two(stiff, strip)
        hard_below = row_below(hard, hard_after)
        hard_right = on_right(hard)
        face_down = 2.0 * hard * hard_below / jnp.maximum(hard + hard_below, 1e-20)
        face_right = 2.0 * hard * hard_right / jnp.maximum(hard + hard_right, 1e-20)
        face_right = jnp.where(lane_in < columns - 1, face_right, 0.0)
        face_dn[pl.ds(begin, 8), :] = face_down
        face_rt[pl.ds(begin, 8), :] = face_right
        here, after = two(loads, strip)
        flux = face_down * (here - row_below(here, after))
        along_rows = flux - row_above(flux, flux_before)
        across = face_right * (here - on_right(here))
        along_columns = across - on_left(across)
        held = ground[pl.ds(begin, 8), :] * here
        one = force0 * (held + along_rows + shear * along_columns)
        other = force1 * (held + shear * along_rows + along_columns)
        image0[pl.ds(begin + PAD, 8), :] = one
        image1[pl.ds(begin + PAD, 8), :] = other
        own = jnp.where(own_rows(strip), here, 0.0)
        return flux, norm + folded(own * own), energy + folded(own * (force0 * one + force1 * other))

    flux, norm, energy = lax.fori_loop(0, strips, first_image, (blank, narrow, narrow), unroll=True)

    def whole_sum(cells):
        return jnp.sum(jnp.sum(cells, axis=0, keepdims=True), axis=1, keepdims=True)

    norm = whole_sum(norm) * (force0 * force0 + force1 * force1)
    energy = whole_sum(energy)
    ratio = jnp.where(norm > 0.0, energy / jnp.where(norm > 0.0, norm, 1.0), 0.0)

    def second_image(strip, carry):
        flux_before, sums = list(carry[:2]), list(carry[2:])
        begin = strip_of(strip)
        face_down = face_dn[pl.ds(begin, 8), :]
        face_right = face_rt[pl.ds(begin, 8), :]
        load, load_after = two(loads, strip)
        held = ground[pl.ds(begin, 8), :]
        keep = own_rows(strip)
        for at, (array, push, of_rows, of_columns) in enumerate((
            (image0, force0, 1.0, shear), (image1, force1, shear, 1.0)
        )):
            image, image_after = two(array, strip)
            lean = ratio * push
            here = image - lean * load
            flux = face_down * (here - row_below(here, image_after - lean * load_after))
            along_rows = flux - row_above(flux, flux_before[at])
            flux_before[at] = flux
            across = face_right * (here - on_right(here))
            along_columns = across - on_left(across)
            applied = held * here + of_rows * along_rows + of_columns * along_columns
            applied = jnp.where(keep, applied, 0.0)
            sums[0] = sums[0] + folded(jnp.where(keep, here * here, 0.0))
            sums[1] = sums[1] + folded(here * applied)
            sums[2] = sums[2] + push * folded(load * applied)
        return tuple(flux_before + sums)

    first_strip = EDGE // 8
    last_strip = (EDGE + rows + 7) // 8
    rest = lax.fori_loop(
        first_strip, last_strip, second_image, (blank, blank, narrow, narrow, narrow), unroll=True
    )[2:]
    values = [norm, ratio] + [whole_sum(cells) for cells in rest]
    lane8 = lax.broadcasted_iota(jnp.int32, (8, LANES), 1)
    packed = jnp.zeros((8, LANES), f32)
    for at, value in enumerate(values):
        packed = jnp.where(lane8 == at, value, packed)
    share[...] = packed

    def share_copy(off):
        return pltpu.make_async_remote_copy(
            src_ref=share,
            dst_ref=shares.at[off - 1],
            send_sem=share_send.at[off - 1],
            recv_sem=share_recv.at[off - 1],
            device_id={"space": lax.rem(me_s + off, n_space)},
            device_id_type=MESH,
        )

    for off in range(1, n_space):
        share_copy(off).start()
    for off in range(1, n_space):
        share_copy(off).wait_recv()
    tables = [packed] + [shares[off - 1] for off in range(1, n_space)]
    lists = [[each[0:1, at:at + 1] for at in range(5)] for each in tables]
    norm_now = sum(each[0] for each in lists)
    centre = sum(each[0] * each[1] for each in lists) / norm_now
    spare = 0.0
    bend = 0.0
    for part_norm, part_ratio, part_spare, part_bend, part_cross in lists:
        shift = part_ratio - centre
        spare = spare + part_spare + shift * shift * part_norm
        bend = bend + part_bend + shift * (part_cross + part_spare) + shift * shift * part_ratio * part_norm
    inverse = 1.0 / centre
    norm_next = spare * inverse * inverse
    renew = norm_next / norm_now
    curve = bend * inverse * inverse - renew * norm_next * centre
    step = norm_next / curve
    of_load = inverse + step * (1.0 + renew)
    of_image = -step * inverse

    def slopes(strip, bend_before):
        begin = strip_of(strip)
        face_down = face_dn[pl.ds(begin, 8), :]
        face_right = face_rt[pl.ds(begin, 8), :]
        load, load_after = two(loads, strip)
        hard = stiff[pl.ds(begin + PAD, 8), :]
        held = jnp.zeros((8, columns), f32)
        bend_down = jnp.zeros((8, columns), f32)
        bend_right = jnp.zeros((8, columns), f32)
        for array, push, of_rows, of_columns in (
            (image0, force0, 1.0, shear), (image1, force1, shear, 1.0)
        ):
            image, image_after = two(array, strip)
            lean = of_load * push
            here = lean * load + of_image * image
            down = here - row_below(here, lean * load_after + of_image * image_after)
            right = here - on_right(here)
            held = held + here * here
            bend_down = bend_down + of_rows * (down * down)
            bend_right = bend_right + of_columns * (right * right)
        bend_down = face_down * face_down * bend_down
        bend_right = face_right * face_right * bend_right
        bent = bend_down + row_above(bend_down, bend_before) + bend_right + on_left(bend_right)
        bent = bent * 0.5 / jnp.maximum(hard * hard, 1e-6)
        gain[pl.ds(begin, 8), :] = factor[pl.ds(begin, 8), :] * (kappa_ground * held + bent)
        return bend_down

    lax.fori_loop(0, strips, slopes, blank, unroll=True)

    for at in range(kernels):
        scale = gain[...]
        sent = jnp.concatenate(
            [fields[at, pl.ds(0, span), :] * scale, -(fields[at, pl.ds(span, span), :] * scale)], axis=0
        )
        hi, lo = halves(sent)
        both = back_row_both[at][:, :2 * span]
        of_high = dot(both, hi)
        turned = of_high[:2 * rows] + of_high[2 * rows:] + dot(both[:2 * rows], lo)
        for part in range(2):
            piece = turned[part * rows:(part + 1) * rows]
            parts = [piece[:, block * LANES:(block + 1) * LANES] for block in range(blocks)]
            for block in range(blocks):
                field = 2 * at + part
                hi, lo = halves(parts[block])
                lanes = pl.ds(field * LANES, LANES)
                back_hi[block, :, lanes] = hi
                back_lo[block, :, lanes] = lo
                edge = side_lanes(parts, block)
                edge_hi = edge.astype(bf16).astype(f32)
                slots = LANES // (2 * radius)
                place = field % slots
                turn = radius + place * 2 * radius
                keep = lane_out // (2 * radius) == place
                for group, cells in ((field // slots, edge_hi), (2 * kernels // slots + field // slots, edge - edge_hi)):
                    moved = pltpu.roll(cells, turn % LANES, 1)
                    lanes = pl.ds(group * LANES, LANES)
                    moved = jnp.where(keep, moved, 0.0 if place == 0 else sides_held[block, :, lanes])
                    if place == slots - 1:
                        lanes = pl.ds((2 * kernels + group) * LANES, LANES)
                        back_hi[block, :, lanes] = moved.astype(bf16)
                    else:
                        sides_held[block, :, lanes] = moved

    width = columns // n_corner
    per_block = LANES // width
    my_block = me_c // per_block

    def term_copy(block, other, sent_as):
        slot = lax.rem(other - me_c + n_corner, n_corner) - 1
        return pltpu.make_async_remote_copy(
            src_ref=term.at[block],
            dst_ref=landed.at[slot],
            send_sem=term_send.at[sent_as],
            recv_sem=term_recv.at[slot],
            device_id={"corner": other},
            device_id_type=MESH,
        )

    sends = []
    half = blocks // 2
    ahead = [half, half - 1, half + 1, half + 2] + [at for at in range(half - 2, 0, -1)]
    ahead += [at for at in range(half + 3, blocks)] + [0]
    for group in (ahead[:half], ahead[half:]):
        places = [lax.rem(my_block + at, blocks) for at in group]
        hi = jnp.concatenate([back_hi[place] for place in places], axis=0)
        lo = jnp.concatenate([back_lo[place] for place in places], axis=0)
        wide = dot(hi, back_col[...])
        value = wide[:, :LANES] + wide[:, LANES:] + dot(lo, back_col[pl.ds(0, 2 * kernels * LANES), pl.ds(0, LANES)])
        for at, place in enumerate(places):
            term[place] = value[at * rows:(at + 1) * rows]
        for at, place in zip(group, places):
            for step in range(per_block):
                if at == 0 and step == 0:
                    continue
                other = place * per_block + lax.rem(me_c + step, per_block)
                copy = term_copy(place, other, len(sends))
                copy.start()
                sends.append(copy)
    summed = term[my_block]
    for off in range(1, n_corner):
        term_copy(my_block, lax.rem(me_c + off, n_corner), off - 1).wait_recv()
        summed = summed + landed[off - 1]
    if per_block == 1:
        out_ref[...] = summed
    else:
        place = lax.rem(me_c, per_block)
        kept = jnp.zeros(out_ref.shape, f32)
        for at in range(per_block):
            kept = kept + jnp.where(place == at, 1.0, 0.0) * summed[:, at * width:(at + 1) * width]
        out_ref[...] = kept

    for copy in sends:
        copy.wait_send()
    for off in range(1, n_space):
        share_copy(off).wait_send()

    @pl.when(has_before)
    def _():
        for copy in edge_copies(0):
            copy.wait_send()

    @pl.when(has_after)
    def _():
        for copy in edge_copies(1):
            copy.wait_send()


def on_device(
    n_space, n_corner,
    design, corner_set, corner_dose, kernel_taps, kernel_weights, support_mask, load_mask, force,
):
    rows, columns = design.shape
    kernels = kernel_taps.shape[2]
    radius = kernel_taps.shape[3] // 2
    span = rows + 2 * EDGE
    reach = rows + 2 * HALO
    blocks = columns // LANES
    padded_rows = span + 2 * PAD
    in_hbm = pl.BlockSpec(memory_space=pltpu.HBM)
    in_vmem = pl.BlockSpec(memory_space=pltpu.VMEM)
    scratch = [
        pltpu.SMEM(corner_set.shape, jnp.int32),
        pltpu.SMEM(corner_dose.shape, f32),
        pltpu.SMEM(kernel_weights.shape, f32),
        pltpu.SMEM(force.shape, f32),
        pltpu.VMEM(design.shape, f32),
        pltpu.VMEM(kernel_taps.shape, f32),
        pltpu.VMEM(design.shape, jnp.int32),
        pltpu.VMEM(design.shape, jnp.int32),
        pltpu.VMEM((4 * kernels, LANES), f32),
        pltpu.VMEM((4 * kernels, LANES), f32),
        pltpu.VMEM((4 * kernels, LANES), f32),
        pltpu.VMEM((kernels, 4 * LANES, 2 * LANES), bf16),
        pltpu.VMEM((2 * kernels * (LANES + 4 * radius), 2 * LANES), bf16),
        pltpu.VMEM((kernels, 4 * span, 2 * LANES), bf16),
        pltpu.VMEM((kernels, 4 * rows, 2 * LANES), bf16),
        pltpu.VMEM((2 * HALO, columns), f32),
        pltpu.VMEM((2, 2 * MASK_HALO, columns), jnp.int32),
        pltpu.VMEM((blocks * rows, 4 * LANES), bf16),
        pltpu.VMEM((kernels, 2 * reach, columns), bf16),
        pltpu.VMEM((kernels, 2 * reach, columns), bf16),
        pltpu.VMEM((kernels, 2 * span, columns), f32),
        pltpu.VMEM((blocks, rows, 2 * kernels * (LANES + 4 * radius)), bf16),
        pltpu.VMEM((blocks, rows, 2 * kernels * LANES), bf16),
        pltpu.VMEM((blocks, rows, 8 * kernels * radius), f32),
        pltpu.VMEM((span, columns), f32),
        pltpu.VMEM((padded_rows, columns), f32),
        pltpu.VMEM((span, columns), f32),
        pltpu.VMEM((padded_rows, columns), f32),
        pltpu.VMEM((span, columns), f32),
        pltpu.VMEM((padded_rows, columns), f32),
        pltpu.VMEM((padded_rows, columns), f32),
        pltpu.VMEM((padded_rows, columns), f32),
        pltpu.VMEM((span, columns), f32),
        pltpu.VMEM((span, columns), f32),
        pltpu.VMEM((blocks, rows, LANES), f32),
        pltpu.VMEM((8, LANES), f32),
        pltpu.VMEM((n_space - 1, 8, LANES), f32),
        pltpu.VMEM((n_corner - 1, rows, LANES), f32),
        pltpu.SemaphoreType.DMA((8,)),
        pltpu.SemaphoreType.DMA((2, 3)),
        pltpu.SemaphoreType.DMA((2, 3)),
        pltpu.SemaphoreType.DMA((n_space - 1,)),
        pltpu.SemaphoreType.DMA((n_space - 1,)),
        pltpu.SemaphoreType.DMA((n_corner - 1,)),
        pltpu.SemaphoreType.DMA((n_corner - 1,)),
    ]
    return pl.pallas_call(
        functools.partial(kernel, n_space, n_corner, kernels, radius),
        out_shape=jax.ShapeDtypeStruct((rows, columns // n_corner), f32),
        in_specs=[in_hbm] * 8,
        out_specs=in_vmem,
        scratch_shapes=scratch,
        compiler_params=pltpu.CompilerParams(
            collective_id=0, has_side_effects=True, vmem_limit_bytes=56 * 1024 * 1024
        ),
    )(
        corner_set, corner_dose, kernel_weights, force,
        design, kernel_taps, support_mask, load_mask,
    )


def solution(mesh):
    placed = (
        P("space", None),
        P("corner"),
        P("corner"),
        P(),
        P(),
        P("space", None),
        P("space", None),
        P(),
    )
    body = functools.partial(on_device, mesh.shape["space"], mesh.shape["corner"])
    return jax.shard_map(
        body, mesh=mesh, in_specs=placed, out_specs=P("space", "corner"), check_vma=False
    )
```
